128 devices in a mesh: samp: 4 (over y_hi, core), par: 32 (over z, x, y_lo).
Axes of the slice: x: 4, y: 4 (y_hi: 2, y_lo: 2; y = y_hi * 2 + y_lo), z: 4, core: 2. Of those that a mesh axis runs over, the one named last changes fastest.
Arguments:
- jacobian: bfloat16 [512, 65536], P('samp', 'par'), as said below
- energies: float32 [512], P('samp'), as said below
Outputs:
- update: float32 [65536], P('par')
- coefficients: float32 [512], P('samp')
Inputs may be any that keep to these rules, and one draw needn't show every extreme that they name: `jacobian`: real log-derivatives; each sample's row and each parameter's column carries its own scale. Real local energies.
All inputs are finite; a program needn't handle non-finite values.
Results may differ from the reference program's by a relative error of at most 0.0049.
Values may be sent and summed in bfloat16 or wider, within the bound.
No kernel may reach another device: no remote copies, remote signals or barrier semaphores. Data moves between devices by JAX's collectives and lax.ppermute only.
A program may use at most 64 MiB of HBM per device.

```python
import math
import jax
import jax.numpy as jnp
from jax import lax

SAMPLES = 512
PARAMS = 65536


def draw_jacobian(key, part):
    key = jax.random.fold_in(key, 11)
    keys = jax.random.split(key, 4)
    ramp = jnp.arange(SAMPLES, dtype=jnp.float32) / max(SAMPLES - 1, 1)
    row_scale = (1.0 + 2.0 * ramp) * jnp.exp(jax.random.uniform(keys[0], (SAMPLES,), jnp.float32, 0.0, math.log(3.0)))
    col_scale = jnp.exp(jax.random.uniform(keys[1], (PARAMS,), jnp.float32, math.log(0.3), math.log(3.0))) / 1.39
    offset = jax.random.normal(keys[2], (PARAMS,), jnp.float32)
    noise = jax.random.normal(keys[3], (SAMPLES, PARAMS), jnp.float32)
    amplitude = math.sqrt(SAMPLES / PARAMS)
    values = amplitude * row_scale[:, None] * col_scale[None, :] * (offset[None, :] + noise)
    return values.astype(jnp.bfloat16)


def draw_energies(key, part):
    key = jax.random.fold_in(key, 23)
    ramp = jnp.arange(SAMPLES, dtype=jnp.float32) / max(SAMPLES - 1, 1)
    noise = jax.random.normal(key, (SAMPLES,), jnp.float32)
    return -2.0 * (1.0 + 2.0 * ramp) + noise


def setup_inputs(seed: int = 0) -> dict:
    streams_of = jax.random.split(jax.random.key(seed), 3)
    jacobian = draw_jacobian(jax.random.fold_in(streams_of[2], 71), 0)
    energies = draw_energies(jax.random.fold_in(streams_of[2], 71), 0)
    return dict(jacobian=jacobian, energies=energies)


def chol_solve(factor, rhs):
    column = rhs[:, None]
    lower_sol = lax.linalg.triangular_solve(factor, column, left_side=True, lower=True)
    upper_sol = lax.linalg.triangular_solve(factor, lower_sol, left_side=True, lower=True, transpose_a=True)
    return upper_sol[:, 0]

def reference(jacobian, energies):
    scale = 1.0 / math.sqrt(SAMPLES)
    column_mean = lax.optimization_barrier(jnp.sum(jacobian, axis=0, dtype=jnp.float32)) / SAMPLES
    centered = ((jacobian.astype(jnp.float32) - column_mean[None, :]) * scale).astype(jnp.bfloat16)
    energy_mean = jnp.sum(energies) / SAMPLES
    centered_energy = (energies - energy_mean) * scale
    gram = jnp.dot(centered.astype(jnp.float32), centered.T.astype(jnp.float32), preferred_element_type=jnp.float32)
    gram = gram + 0.05 * jnp.eye(SAMPLES, dtype=jnp.float32)
    factor = jnp.linalg.cholesky(gram)
    coefficients = chol_solve(factor, centered_energy)
    update = jnp.dot(coefficients, centered.astype(jnp.float32), precision=lax.Precision.HIGHEST)
    update = update * math.sqrt(PARAMS)
    return (update, coefficients)
```

```python
import math

import jax
import jax.numpy as jnp
from jax import lax
from jax.experimental import pallas as pl
from jax.experimental.pallas import tpu as pltpu
from jax.sharding import Mesh, PartitionSpec as P

GROUP = 128
ROWS = 8
PANELS = GROUP // ROWS
RIDGE = 0.05


def center_gram_kernel(place_ref, a_ref, b_ref, c_ref, d_ref, cent_ref, out_ref):
    total = 4 * GROUP
    scale = 1.0 / math.sqrt(total)
    parts = (a_ref, b_ref, c_ref, d_ref)
    column_sum = None
    for part in parts:
        piece = jnp.sum(part[...].astype(jnp.float32), axis=0, keepdims=True)
        column_sum = piece if column_sum is None else column_sum + piece
    mean = column_sum / total
    for number, part in enumerate(parts):
        start = pl.multiple_of(place_ref[number] * GROUP, GROUP)
        cent_ref[pl.ds(start, GROUP), :] = (
            (part[...].astype(jnp.float32) - mean) * scale
        ).astype(jnp.bfloat16)
    half = total // 2
    start = pl.multiple_of(place_ref[4] * half, half)
    gram = lax.dot_general(
        cent_ref[pl.ds(start, half), :],
        cent_ref[...],
        (((1,), (1,)), ((), ())),
        preferred_element_type=jnp.float32,
    )
    for strip in range(half // ROWS):
        for side in range(2):
            out_ref[2 * strip + side] = gram[
                ROWS * strip : ROWS * strip + ROWS, half * side : half * side + half
            ]


def lane(value, index):
    return jnp.broadcast_to(value[:, index : index + 1], (ROWS, GROUP))


def row(value, index):
    return jnp.broadcast_to(value[index : index + 1, :], (ROWS, GROUP))


def factor_block(rows):
    rows = list(rows)
    column = lax.broadcasted_iota(jnp.int32, (ROWS, GROUP), 1)
    line = lax.broadcasted_iota(jnp.int32, (ROWS, GROUP), 0)
    inverse, recips = [], []
    for p in range(PANELS):
        first = ROWS * p
        own = (column >= first) & (column < first + ROWS)
        panel = rows[p]
        spread = [lane(panel, first + j) for j in range(ROWS)]
        pivot = {(i, j): row(spread[j], i) for j in range(ROWS) for i in range(j, ROWS)}
        panel = jnp.where(own, (column - first == line).astype(jnp.float32), panel)
        work = [row(panel, i) for i in range(ROWS)]
        recip, lower = [], {}
        for j in range(ROWS):
            recip.append(1.0 / pivot[j, j])
            for i in range(j + 1, ROWS):
                lower[i, j] = pivot[i, j] * recip[j]
            for i in range(j + 1, ROWS):
                for m in range(j + 1, i + 1):
                    pivot[i, m] = pivot[i, m] - lower[i, j] * pivot[m, j]
                work[i] = work[i] - lower[i, j] * work[j]
        done = work[0]
        scale = recip[0]
        for j in range(1, ROWS):
            done = jnp.where(line == j, work[j], done)
            scale = jnp.where(line == j, recip[j], scale)
        inverse.append(jnp.where(column < first + ROWS, done, 0.0))
        recips.append(scale)
        if p == PANELS - 1:
            break
        solved = [work[j] * recip[j] for j in range(ROWS)]
        for j in range(ROWS - 1, -1, -1):
            for i in range(j):
                solved[i] = solved[i] - lower[j, i] * solved[j]
        for i in range(p + 1, PANELS):
            value = jnp.where(own, 0.0, rows[i])
            for j in range(ROWS):
                value = value - lane(rows[i], first + j) * solved[j]
            rows[i] = value
    return inverse, recips


def product(left, right, dims):
    return lax.dot_general(
        left,
        right,
        (dims, ((), ())),
        precision=lax.Precision.HIGHEST,
        preferred_element_type=jnp.float32,
    )


def solve_kernel(
    place_ref, mine_ref, other_ref, rhs_ref, cent_ref, coeff_ref, update_ref, gram, low, rec, z
):
    blocks = 4
    core = place_ref[4]
    for strip in range(2 * PANELS):
        for side in range(2):
            for which, ref in ((core, mine_ref), (1 - core, other_ref)):
                block_row = 2 * which + strip // PANELS
                inner = ROWS * (strip % PANELS)
                for part in range(2):
                    gram[block_row, 2 * side + part, inner : inner + ROWS, :] = ref[
                        2 * strip + side, :, GROUP * part : GROUP * part + GROUP
                    ]
    for k in range(blocks):
        gram[k, blocks] = rhs_ref[GROUP * k : GROUP * k + GROUP, :]
    column = lax.broadcasted_iota(jnp.int32, (ROWS, GROUP), 1)
    line = lax.broadcasted_iota(jnp.int32, (ROWS, GROUP), 0)

    def step(k, carry):
        panels = []
        for p in range(PANELS):
            ridge = jnp.where(column - ROWS * p == line, RIDGE, 0.0)
            panels.append(gram[k, k, ROWS * p : ROWS * p + ROWS, :] + ridge)
        inverse, recips = factor_block(panels)
        for p in range(PANELS):
            low[k, ROWS * p : ROWS * p + ROWS, :] = inverse[p]
            rec[k, ROWS * p : ROWS * p + ROWS, :] = recips[p]
        for now in range(blocks):

            @pl.when(k == now)
            def _():
                tri = low[now]
                rc = rec[now]
                ys = {j: product(tri, gram[now, j], ((1,), (0,))) for j in range(now + 1, blocks + 1)}
                zs = {j: ys[j] * rc for j in ys}
                for j in zs:
                    z[now, j] = zs[j]
                for i in range(now + 1, blocks):
                    for j in range(i, blocks + 1):
                        gram[i, j] = gram[i, j] - product(ys[i], zs[j], ((0,), (0,)))

        return carry

    lax.fori_loop(0, blocks, step, 0)
    xs = [None] * blocks
    for k in range(blocks - 1, -1, -1):
        right = z[k, blocks]
        for j in range(k + 1, blocks):
            right = right - product(z[k, j], xs[j], ((1,), (0,)))
        xs[k] = product(low[k], right, ((0,), (0,)))
        coeff_ref[GROUP * k : GROUP * k + GROUP, :] = xs[k]
    width = cent_ref.shape[1]
    for piece in range(width // GROUP):
        total = jnp.zeros((ROWS, GROUP), jnp.float32)
        for k in range(blocks):
            values = cent_ref[
                GROUP * k : GROUP * k + GROUP, GROUP * piece : GROUP * piece + GROUP
            ].astype(jnp.float32)
            scaled = values * xs[k]
            total = total + jnp.sum(scaled.reshape(PANELS, ROWS, GROUP), axis=0)
        update_ref[:, GROUP * piece : GROUP * piece + GROUP] = jnp.sum(
            total, axis=0, keepdims=True
        )


VMEM = pl.BlockSpec(memory_space=pltpu.VMEM)
SMEM = pl.BlockSpec(memory_space=pltpu.SMEM)


def center_gram(place, parts):
    columns = parts[0].shape[1]
    return pl.pallas_call(
        center_gram_kernel,
        out_shape=(
            jax.ShapeDtypeStruct((4 * GROUP, columns), jnp.bfloat16),
            jax.ShapeDtypeStruct((64, ROWS, 2 * GROUP), jnp.float32),
        ),
        in_specs=[SMEM] + [VMEM] * 4,
        out_specs=(VMEM, VMEM),
        compiler_params=pltpu.CompilerParams(vmem_limit_bytes=32 * 1024 * 1024),
        name="center_gram",
    )(place, *parts)


def solve(place, mine, other, rhs, cent):
    return pl.pallas_call(
        solve_kernel,
        out_shape=(
            jax.ShapeDtypeStruct((4 * GROUP, GROUP), jnp.float32),
            jax.ShapeDtypeStruct((1, cent.shape[1]), jnp.float32),
        ),
        in_specs=[SMEM] + [VMEM] * 4,
        out_specs=(VMEM, VMEM),
        scratch_shapes=[
            pltpu.VMEM((4, 5, GROUP, GROUP), jnp.float32),
            pltpu.VMEM((4, GROUP, GROUP), jnp.float32),
            pltpu.VMEM((4, GROUP, GROUP), jnp.float32),
            pltpu.VMEM((4, 5, GROUP, GROUP), jnp.float32),
        ],
        compiler_params=pltpu.CompilerParams(vmem_limit_bytes=32 * 1024 * 1024),
        name="solve",
    )(place, mine, other, rhs, cent)


SWAP = [(0, 1), (1, 0)]


def per_device(jacobian, energies):
    high = lax.axis_index("high")
    core = lax.axis_index("core")
    total = 4 * GROUP
    half = jacobian.shape[1] // 2
    keep = lax.dynamic_slice_in_dim(jacobian, high * half, half, 1)
    send = lax.dynamic_slice_in_dim(jacobian, (1 - high) * half, half, 1)
    far = lax.ppermute(send, "high", SWAP)
    far_energy = lax.ppermute(energies, "high", SWAP)
    near = lax.ppermute(keep, "core", SWAP)
    both = jnp.stack([energies, far_energy])
    near_both = lax.ppermute(both, "core", SWAP)
    diagonal = lax.ppermute(far, "core", SWAP)
    order = jnp.stack(
        [2 * high + core, 2 * (1 - high) + core, 2 * high + 1 - core, 2 * (1 - high) + 1 - core]
    )
    place = jnp.concatenate([order, core[None]]).astype(jnp.int32)
    pieces = jnp.concatenate([both, near_both])
    table = jnp.stack([pieces[2 * (g % 2 != core) + (g // 2 != high)] for g in range(4)])
    energy = table.reshape(total)
    centered_energy = (energy - jnp.sum(energy) / total) * (1.0 / math.sqrt(total))
    rhs = jnp.broadcast_to(centered_energy[:, None], (total, GROUP))
    cent, partial = center_gram(place, (keep, far, near, diagonal))
    ring = ("high", "par")
    parts = lax.all_to_all(partial, ring, split_axis=0, concat_axis=0, tiled=True)
    summed = jnp.sum(parts, axis=0)
    mine = lax.all_to_all(
        jnp.broadcast_to(summed[None], parts.shape), ring, split_axis=0, concat_axis=0, tiled=True
    )
    other = lax.ppermute(mine, "core", SWAP)
    coeffs, update = solve(place, mine, other, rhs, cent)
    own = lax.dynamic_slice_in_dim(coeffs, (2 * high + core) * GROUP, GROUP, 0)[:, 0]
    update = update[0] * math.sqrt(2 * half * lax.axis_size("par"))
    away = lax.ppermute(update, "high", SWAP)
    lower = jnp.where(high == 0, update, away)
    upper = jnp.where(high == 0, away, update)
    return jnp.concatenate([lower, upper]), own


def solution(mesh):
    shape = mesh.devices.shape
    fine = Mesh(mesh.devices.reshape(2, 2, shape[1]), ("high", "core", "par"))
    return jax.shard_map(
        per_device,
        mesh=fine,
        in_specs=(P(("high", "core"), "par"), P(("high", "core"))),
        out_specs=(P("par"), P(("high", "core"))),
        check_vma=False,
    )
```

```python
import math

import jax
import jax.numpy as jnp
from jax import lax
from jax.experimental import pallas as pl
from jax.experimental.pallas import tpu as pltpu
from jax.sharding import Mesh, PartitionSpec as P

GROUP = 128
ROWS = 8
PANELS = GROUP // ROWS
RIDGE = 0.05


def center_gram_kernel(place_ref, e_ref, a_ref, b_ref, c_ref, d_ref, cent_ref, out_ref):
    total = 4 * GROUP
    scale = 1.0 / math.sqrt(total)
    parts = (a_ref, b_ref, c_ref, d_ref)
    column_sum = None
    for part in parts:
        piece = jnp.sum(part[...].astype(jnp.float32), axis=0, keepdims=True)
        column_sum = piece if column_sum is None else column_sum + piece
    mean = column_sum / total
    for number, part in enumerate(parts):
        start = pl.multiple_of(place_ref[number] * GROUP, GROUP)
        cent_ref[pl.ds(start, GROUP), :] = (
            (part[...].astype(jnp.float32) - mean) * scale
        ).astype(jnp.bfloat16)
    half = total // 2
    start = pl.multiple_of(place_ref[4] * half, half)
    gram = lax.dot_general(
        cent_ref[pl.ds(start, half), :],
        cent_ref[...],
        (((1,), (1,)), ((), ())),
        preferred_element_type=jnp.float32,
    )
    for strip in range(half // ROWS):
        for side in range(2):
            out_ref[2 * strip + side] = gram[
                ROWS * strip : ROWS * strip + ROWS, half * side : half * side + half
            ]
    column = lax.broadcasted_iota(jnp.int32, (ROWS, GROUP), 1)
    mine = (column // (GROUP // 2) == place_ref[5]) & (place_ref[6] == 0)
    for strip in range(PANELS):
        energies = e_ref[ROWS * strip : ROWS * strip + ROWS, :]
        out_ref[2 * (PANELS + strip), :, :GROUP] = jnp.where(mine, energies, 0.0)


def lane(value, index):
    return jnp.broadcast_to(value[:, index : index + 1], (ROWS, GROUP))


def row(value, index):
    return jnp.broadcast_to(value[index : index + 1, :], (ROWS, GROUP))


def factor_block(rows):
    rows = list(rows)
    column = lax.broadcasted_iota(jnp.int32, (ROWS, GROUP), 1)
    line = lax.broadcasted_iota(jnp.int32, (ROWS, GROUP), 0)
    inverse, recips = [], []
    for p in range(PANELS):
        first = ROWS * p
        own = (column >= first) & (column < first + ROWS)
        panel = rows[p]
        spread = [lane(panel, first + j) for j in range(ROWS)]
        pivot = {(i, j): row(spread[j], i) for j in range(ROWS) for i in range(j, ROWS)}
        panel = jnp.where(own, (column - first == line).astype(jnp.float32), panel)
        work = [row(panel, i) for i in range(ROWS)]
        recip, lower = [], {}
        for j in range(ROWS):
            recip.append(1.0 / pivot[j, j])
            for i in range(j + 1, ROWS):
                lower[i, j] = pivot[i, j] * recip[j]
            for i in range(j + 1, ROWS):
                for m in range(j + 1, i + 1):
                    pivot[i, m] = pivot[i, m] - lower[i, j] * pivot[m, j]
                work[i] = work[i] - lower[i, j] * work[j]
        done = work[0]
        scale = recip[0]
        for j in range(1, ROWS):
            done = jnp.where(line == j, work[j], done)
            scale = jnp.where(line == j, recip[j], scale)
        inverse.append(jnp.where(column < first + ROWS, done, 0.0))
        recips.append(scale)
        if p == PANELS - 1:
            break
        solved = [work[j] * recip[j] for j in range(ROWS)]
        for j in range(ROWS - 1, -1, -1):
            for i in range(j):
                solved[i] = solved[i] - lower[j, i] * solved[j]
        for i in range(p + 1, PANELS):
            value = jnp.where(own, 0.0, rows[i])
            for j in range(ROWS):
                value = value - lane(rows[i], first + j) * solved[j]
            rows[i] = value
    return inverse, recips


def product(left, right, dims):
    return lax.dot_general(
        left,
        right,
        (dims, ((), ())),
        precision=lax.Precision.HIGHEST,
        preferred_element_type=jnp.float32,
    )


def solve_kernel(
    place_ref, mine_ref, other_ref, cent_ref, coeff_ref, update_ref, gram, low, rec, z
):
    blocks = 4
    core = place_ref[4]
    for strip in range(2 * PANELS):
        for side in range(2):
            for which, ref in ((core, mine_ref), (1 - core, other_ref)):
                block_row = 2 * which + strip // PANELS
                inner = ROWS * (strip % PANELS)
                for part in range(2):
                    gram[block_row, 2 * side + part, inner : inner + ROWS, :] = ref[
                        2 * strip + side, :, GROUP * part : GROUP * part + GROUP
                    ]
    energy_sum = jnp.zeros((ROWS, GROUP), jnp.float32)
    for which, ref in ((core, mine_ref), (1 - core, other_ref)):
        for high in range(2):
            for p in range(PANELS):
                value = lane(ref[2 * (PANELS + p), :, :GROUP], high * GROUP // 2)
                gram[2 * high + which, blocks, ROWS * p : ROWS * p + ROWS, :] = value
                energy_sum = energy_sum + value
    energy_mean = jnp.sum(energy_sum, axis=0, keepdims=True) / (blocks * GROUP)
    scale = 1.0 / math.sqrt(blocks * GROUP)
    for k in range(blocks):
        gram[k, blocks] = (gram[k, blocks] - energy_mean) * scale
    column = lax.broadcasted_iota(jnp.int32, (ROWS, GROUP), 1)
    line = lax.broadcasted_iota(jnp.int32, (ROWS, GROUP), 0)

    def step(k, carry):
        panels = []
        for p in range(PANELS):
            ridge = jnp.where(column - ROWS * p == line, RIDGE, 0.0)
            panels.append(gram[k, k, ROWS * p : ROWS * p + ROWS, :] + ridge)
        inverse, recips = factor_block(panels)
        for p in range(PANELS):
            low[k, ROWS * p : ROWS * p + ROWS, :] = inverse[p]
            rec[k, ROWS * p : ROWS * p + ROWS, :] = recips[p]
        for now in range(blocks):

            @pl.when(k == now)
            def _():
                tri = low[now]
                rc = rec[now]
                ys = {j: product(tri, gram[now, j], ((1,), (0,))) for j in range(now + 1, blocks + 1)}
                zs = {j: ys[j] * rc for j in ys}
                for j in zs:
                    z[now, j] = zs[j]
                for i in range(now + 1, blocks):
                    for j in range(i, blocks + 1):
                        gram[i, j] = gram[i, j] - product(ys[i], zs[j], ((0,), (0,)))

        return carry

    lax.fori_loop(0, blocks, step, 0)
    xs = [None] * blocks
    for k in range(blocks - 1, -1, -1):
        right = z[k, blocks]
        for j in range(k + 1, blocks):
            right = right - product(z[k, j], xs[j], ((1,), (0,)))
        xs[k] = product(low[k], right, ((0,), (0,)))
        coeff_ref[GROUP * k : GROUP * k + GROUP, :] = xs[k]
    width = cent_ref.shape[1]
    for piece in range(width // GROUP):
        total = jnp.zeros((ROWS, GROUP), jnp.float32)
        for k in range(blocks):
            values = cent_ref[
                GROUP * k : GROUP * k + GROUP, GROUP * piece : GROUP * piece + GROUP
            ].astype(jnp.float32)
            scaled = values * xs[k]
            total = total + jnp.sum(scaled.reshape(PANELS, ROWS, GROUP), axis=0)
        update_ref[:, GROUP * piece : GROUP * piece + GROUP] = jnp.sum(
            total, axis=0, keepdims=True
        )


VMEM = pl.BlockSpec(memory_space=pltpu.VMEM)
SMEM = pl.BlockSpec(memory_space=pltpu.SMEM)


def center_gram(place, energies, parts):
    columns = parts[0].shape[1]
    return pl.pallas_call(
        center_gram_kernel,
        out_shape=(
            jax.ShapeDtypeStruct((4 * GROUP, columns), jnp.bfloat16),
            jax.ShapeDtypeStruct((64, ROWS, 2 * GROUP), jnp.float32),
        ),
        in_specs=[SMEM] + [VMEM] * 5,
        out_specs=(VMEM, VMEM),
        compiler_params=pltpu.CompilerParams(vmem_limit_bytes=32 * 1024 * 1024),
        name="center_gram",
    )(place, energies, *parts)


def solve(place, mine, other, cent):
    return pl.pallas_call(
        solve_kernel,
        out_shape=(
            jax.ShapeDtypeStruct((4 * GROUP, GROUP), jnp.float32),
            jax.ShapeDtypeStruct((1, cent.shape[1]), jnp.float32),
        ),
        in_specs=[SMEM] + [VMEM] * 3,
        out_specs=(VMEM, VMEM),
        scratch_shapes=[
            pltpu.VMEM((4, 5, GROUP, GROUP), jnp.float32),
            pltpu.VMEM((4, GROUP, GROUP), jnp.float32),
            pltpu.VMEM((4, GROUP, GROUP), jnp.float32),
            pltpu.VMEM((4, 5, GROUP, GROUP), jnp.float32),
        ],
        compiler_params=pltpu.CompilerParams(vmem_limit_bytes=32 * 1024 * 1024),
        name="solve",
    )(place, mine, other, cent)


SWAP = [(0, 1), (1, 0)]


def per_device(jacobian, energies):
    high = lax.axis_index("high")
    core = lax.axis_index("core")
    half = jacobian.shape[1] // 2
    keep = lax.dynamic_slice_in_dim(jacobian, high * half, half, 1)
    send = lax.dynamic_slice_in_dim(jacobian, (1 - high) * half, half, 1)
    far = lax.ppermute(send, "high", SWAP)
    near = lax.ppermute(keep, "core", SWAP)
    diagonal = lax.ppermute(far, "core", SWAP)
    place = jnp.stack(
        [
            2 * high + core,
            2 * (1 - high) + core,
            2 * high + 1 - core,
            2 * (1 - high) + 1 - core,
            core,
            high,
            lax.axis_index("par"),
        ]
    ).astype(jnp.int32)
    spread = jnp.broadcast_to(energies[:, None], (GROUP, GROUP))
    cent, partial = center_gram(place, spread, (keep, far, near, diagonal))
    ring = ("high", "par")
    parts = lax.all_to_all(partial, ring, split_axis=0, concat_axis=0, tiled=True)
    summed = jnp.sum(parts, axis=0)
    mine = lax.all_to_all(
        jnp.broadcast_to(summed[None], parts.shape), ring, split_axis=0, concat_axis=0, tiled=True
    )
    other = lax.ppermute(mine, "core", SWAP)
    coeffs, update = solve(place, mine, other, cent)
    own = lax.dynamic_slice_in_dim(coeffs, (2 * high + core) * GROUP, GROUP, 0)[:, 0]
    update = update[0] * math.sqrt(2 * half * lax.axis_size("par"))
    away = lax.ppermute(update, "high", SWAP)
    lower = jnp.where(high == 0, update, away)
    upper = jnp.where(high == 0, away, update)
    return jnp.concatenate([lower, upper]), own


def solution(mesh):
    shape = mesh.devices.shape
    fine = Mesh(mesh.devices.reshape(2, 2, shape[1]), ("high", "core", "par"))
    return jax.shard_map(
        per_device,
        mesh=fine,
        in_specs=(P(("high", "core"), "par"), P(("high", "core"))),
        out_specs=(P("par"), P(("high", "core"))),
        check_vma=False,
    )
```

```python
import math

import jax
import jax.numpy as jnp
from jax import lax
from jax.experimental import pallas as pl
from jax.experimental.pallas import tpu as pltpu
from jax.sharding import Mesh, PartitionSpec as P

GROUP = 128
ROWS = 8
WIDE = 2
PANELS = GROUP // ROWS
RIDGE = 0.05


def center_gram_kernel(place_ref, e_ref, a_ref, b_ref, c_ref, d_ref, cent_ref, out_ref):
    total = 4 * GROUP
    scale = 1.0 / math.sqrt(total)
    parts = (a_ref, b_ref, c_ref, d_ref)
    column_sum = None
    for part in parts:
        piece = jnp.sum(part[...].astype(jnp.float32), axis=0, keepdims=True)
        column_sum = piece if column_sum is None else column_sum + piece
    mean = column_sum / total
    for number, part in enumerate(parts):
        start = pl.multiple_of(place_ref[number] * GROUP, GROUP)
        cent_ref[pl.ds(start, GROUP), :] = (
            (part[...].astype(jnp.float32) - mean) * scale
        ).astype(jnp.bfloat16)
    half = total // 2
    start = pl.multiple_of(place_ref[4] * half, half)
    gram = lax.dot_general(
        cent_ref[pl.ds(start, half), :],
        cent_ref[...],
        (((1,), (1,)), ((), ())),
        preferred_element_type=jnp.float32,
    )
    for strip in range(half // ROWS):
        for side in range(2):
            out_ref[2 * strip + side] = gram[
                ROWS * strip : ROWS * strip + ROWS, half * side : half * side + half
            ]
    column = lax.broadcasted_iota(jnp.int32, (ROWS, GROUP), 1)
    mine = (column // (GROUP // 2) == place_ref[5]) & (place_ref[6] == 0)
    for strip in range(PANELS):
        energies = e_ref[ROWS * strip : ROWS * strip + ROWS, :]
        out_ref[2 * (PANELS + strip), :, :GROUP] = jnp.where(mine, energies, 0.0)


def lane(value, index):
    return jnp.broadcast_to(value[:, index : index + 1], (ROWS, GROUP))


def row(value, index):
    return jnp.broadcast_to(value[index : index + 1, :], (ROWS, GROUP))


def factor_block(rows):
    rows = list(rows)
    column = lax.broadcasted_iota(jnp.int32, (ROWS, GROUP), 1)
    line = lax.broadcasted_iota(jnp.int32, (ROWS, GROUP), 0)
    size = WIDE * ROWS
    inverse, recips = [], []
    for p in range(0, PANELS, WIDE):
        first = ROWS * p
        after = list(range(p + WIDE, min(p + 2 * WIDE, PANELS)))
        beyond = list(range(p + 2 * WIDE, PANELS))
        own = (column >= first) & (column < first + size)
        held = {
            (m, t): lane(rows[p + t], first + m) for m in range(size) for t in range(m // ROWS, WIDE)
        }
        next_held = {(m, i): lane(rows[i], first + m) for m in range(size) for i in after}
        work = [
            jnp.where(own, (column - first - ROWS * t == line).astype(jnp.float32), rows[p + t])
            for t in range(WIDE)
        ]
        following = {i: jnp.where(own, 0.0, rows[i]) for i in after}
        scale = [None] * WIDE
        for j in range(size):
            home, at = divmod(j, ROWS)
            pivot_row = row(work[home], at)
            spread = {m: row(held[j, m // ROWS], m % ROWS) for m in range(j, size)}
            recip = 1.0 / spread[j]
            scale[home] = recip if at == 0 else jnp.where(line == at, recip, scale[home])
            factor = {t: held[j, t] * recip for t in range(home, WIDE)}
            for m in range(j + 1, size):
                for t in range(m // ROWS, WIDE):
                    if m == j + 1:
                        held[m, t] = held[m, t] - (held[j, t] * spread[m]) * recip
                    else:
                        held[m, t] = held[m, t] - factor[t] * spread[m]
            for t in range(home, WIDE):
                part = jnp.where(line > at, factor[t], 0.0) if t == home else factor[t]
                work[t] = work[t] - part * pivot_row
            for i in after:
                part = next_held[j, i] * recip
                for m in range(j + 1, size):
                    next_held[m, i] = next_held[m, i] - part * spread[m]
                following[i] = following[i] - part * pivot_row
        for t in range(WIDE):
            inverse.append(jnp.where(column < first + size, work[t], 0.0))
            recips.append(scale[t])
        for i in after:
            rows[i] = following[i]
        if beyond:
            panel = jnp.concatenate(work, axis=0)
            scaled = jnp.concatenate([work[t] * scale[t] for t in range(WIDE)], axis=0)
            change = contract(stack_left(scaled, 0), stack_right(panel, 0), 0)
            for i in beyond:
                change_tile = change[ROWS * i : ROWS * i + ROWS, :]
                rows[i] = jnp.where(own, 0.0, rows[i]) - change_tile
    return inverse, recips


def split(value):
    high = value.astype(jnp.bfloat16)
    rest = value - high.astype(jnp.float32)
    middle = rest.astype(jnp.bfloat16)
    return high, middle, (rest - middle.astype(jnp.float32)).astype(jnp.bfloat16)


def stack_left(value, axis):
    high, middle, low = split(value)
    return jnp.concatenate([high, high, middle, middle, high, low], axis=axis)


def stack_right(value, axis):
    high, middle, low = split(value)
    return jnp.concatenate([high, middle, high, middle, low, high], axis=axis)


def contract(left, right, axis):
    return lax.dot_general(
        left, right, (((axis,), (0,)), ((), ())), preferred_element_type=jnp.float32
    )


def solve_kernel(
    place_ref, mine_ref, other_ref, cent_ref, coeff_ref, update_ref, gram, low, rec, z
):
    blocks = 4
    core = place_ref[4]
    for strip in range(2 * PANELS):
        for side in range(2):
            for which, ref in ((core, mine_ref), (1 - core, other_ref)):
                block_row = 2 * which + strip // PANELS
                inner = ROWS * (strip % PANELS)
                for part in range(2):
                    gram[block_row, 2 * side + part, inner : inner + ROWS, :] = ref[
                        2 * strip + side, :, GROUP * part : GROUP * part + GROUP
                    ]
    energy_sum = jnp.zeros((ROWS, GROUP), jnp.float32)
    for which, ref in ((core, mine_ref), (1 - core, other_ref)):
        for high in range(2):
            for p in range(PANELS):
                value = lane(ref[2 * (PANELS + p), :, :GROUP], high * GROUP // 2)
                gram[2 * high + which, blocks, ROWS * p : ROWS * p + ROWS, :] = value
                energy_sum = energy_sum + value
    energy_mean = jnp.sum(energy_sum, axis=0, keepdims=True) / (blocks * GROUP)
    scale = 1.0 / math.sqrt(blocks * GROUP)
    for k in range(blocks):
        gram[k, blocks] = (gram[k, blocks] - energy_mean) * scale
    column = lax.broadcasted_iota(jnp.int32, (ROWS, GROUP), 1)
    line = lax.broadcasted_iota(jnp.int32, (ROWS, GROUP), 0)

    def step(k):
        panels = []
        for p in range(PANELS):
            ridge = jnp.where(column - ROWS * p == line, RIDGE, 0.0)
            panels.append(gram[k, k, ROWS * p : ROWS * p + ROWS, :] + ridge)
        inverse, recips = factor_block(panels)
        for p in range(PANELS):
            low[k, ROWS * p : ROWS * p + ROWS, :] = inverse[p]
            rec[k, ROWS * p : ROWS * p + ROWS, :] = recips[p]
        tri = stack_left(low[k], 1)
        later = range(k + 1, blocks + 1)
        ys = {j: contract(tri, stack_right(gram[k, j], 0), 1) for j in later}
        zs = {j: ys[j] * rec[k] for j in later}
        for j in later:
            z[k, j] = zs[j]
        right = {j: stack_right(zs[j], 0) for j in later}
        for i in range(k + 1, blocks):
            left = stack_left(ys[i], 0)
            for j in range(i, blocks + 1):
                gram[i, j] = gram[i, j] - contract(left, right[j], 0)

    for k in range(blocks):
        step(k)
    xs = [None] * blocks
    spread = [None] * blocks
    for k in range(blocks - 1, -1, -1):
        right = z[k, blocks]
        for j in range(k + 1, blocks):
            right = right - contract(stack_left(z[k, j], 1), spread[j], 1)
        xs[k] = contract(stack_left(low[k], 0), stack_right(right, 0), 0)
        spread[k] = stack_right(xs[k], 0)
        coeff_ref[GROUP * k : GROUP * k + GROUP, :] = xs[k]
    width = cent_ref.shape[1]
    for piece in range(width // GROUP):
        total = jnp.zeros((ROWS, GROUP), jnp.float32)
        for k in range(blocks):
            values = cent_ref[
                GROUP * k : GROUP * k + GROUP, GROUP * piece : GROUP * piece + GROUP
            ].astype(jnp.float32)
            scaled = values * xs[k]
            total = total + jnp.sum(scaled.reshape(PANELS, ROWS, GROUP), axis=0)
        update_ref[:, GROUP * piece : GROUP * piece + GROUP] = jnp.sum(
            total, axis=0, keepdims=True
        )


VMEM = pl.BlockSpec(memory_space=pltpu.VMEM)
SMEM = pl.BlockSpec(memory_space=pltpu.SMEM)


def center_gram(place, energies, parts):
    columns = parts[0].shape[1]
    return pl.pallas_call(
        center_gram_kernel,
        out_shape=(
            jax.ShapeDtypeStruct((4 * GROUP, columns), jnp.bfloat16),
            jax.ShapeDtypeStruct((64, ROWS, 2 * GROUP), jnp.float32),
        ),
        in_specs=[SMEM] + [VMEM] * 5,
        out_specs=(VMEM, VMEM),
        compiler_params=pltpu.CompilerParams(vmem_limit_bytes=32 * 1024 * 1024),
        name="center_gram",
    )(place, energies, *parts)


def solve(place, mine, other, cent):
    return pl.pallas_call(
        solve_kernel,
        out_shape=(
            jax.ShapeDtypeStruct((4 * GROUP, GROUP), jnp.float32),
            jax.ShapeDtypeStruct((1, cent.shape[1]), jnp.float32),
        ),
        in_specs=[SMEM] + [VMEM] * 3,
        out_specs=(VMEM, VMEM),
        scratch_shapes=[
            pltpu.VMEM((4, 5, GROUP, GROUP), jnp.float32),
            pltpu.VMEM((4, GROUP, GROUP), jnp.float32),
            pltpu.VMEM((4, GROUP, GROUP), jnp.float32),
            pltpu.VMEM((4, 5, GROUP, GROUP), jnp.float32),
        ],
        compiler_params=pltpu.CompilerParams(vmem_limit_bytes=32 * 1024 * 1024),
        name="solve",
    )(place, mine, other, cent)


SWAP = [(0, 1), (1, 0)]


def per_device(jacobian, energies):
    high = lax.axis_index("high")
    core = lax.axis_index("core")
    half = jacobian.shape[1] // 2
    keep = lax.dynamic_slice_in_dim(jacobian, high * half, half, 1)
    send = lax.dynamic_slice_in_dim(jacobian, (1 - high) * half, half, 1)
    far = lax.ppermute(send, "high", SWAP)
    near = lax.ppermute(keep, "core", SWAP)
    diagonal = lax.ppermute(far, "core", SWAP)
    place = jnp.stack(
        [
            2 * high + core,
            2 * (1 - high) + core,
            2 * high + 1 - core,
            2 * (1 - high) + 1 - core,
            core,
            high,
            lax.axis_index("par"),
        ]
    ).astype(jnp.int32)
    spread = jnp.broadcast_to(energies[:, None], (GROUP, GROUP))
    cent, partial = center_gram(place, spread, (keep, far, near, diagonal))
    ring = ("high", "par")
    parts = lax.all_to_all(partial, ring, split_axis=0, concat_axis=0, tiled=True)
    summed = jnp.sum(parts, axis=0)
    mine = lax.all_to_all(
        jnp.broadcast_to(summed[None], parts.shape), ring, split_axis=0, concat_axis=0, tiled=True
    )
    other = lax.ppermute(mine, "core", SWAP)
    coeffs, update = solve(place, mine, other, cent)
    own = lax.dynamic_slice_in_dim(coeffs, (2 * high + core) * GROUP, GROUP, 0)[:, 0]
    update = update[0] * math.sqrt(2 * half * lax.axis_size("par"))
    away = lax.ppermute(update, "high", SWAP)
    lower = jnp.where(high == 0, update, away)
    upper = jnp.where(high == 0, away, update)
    return jnp.concatenate([lower, upper]), own


def solution(mesh):
    shape = mesh.devices.shape
    fine = Mesh(mesh.devices.reshape(2, 2, shape[1]), ("high", "core", "par"))
    return jax.shard_map(
        per_device,
        mesh=fine,
        in_specs=(P(("high", "core"), "par"), P(("high", "core"))),
        out_specs=(P("par"), P(("high", "core"))),
        check_vma=False,
    )
```

```python
import math

import jax
import jax.numpy as jnp
from jax import lax
from jax.experimental import pallas as pl
from jax.experimental.pallas import tpu as pltpu
from jax.sharding import Mesh, PartitionSpec as P

GROUP = 128
ROWS = 8
WIDE = 2
PANELS = GROUP // ROWS
RIDGE = 0.05


BLOCKS = 4
STRIPS = (((0, 0, 4), (1, 1, 1)), ((1, 2, 2), (2, 2, 2), (3, 3, 1)))
LISTS = tuple(tuple((r, c + n) for r, c, w in strips for n in range(w)) for strips in STRIPS)
HELD = len(LISTS[0]) + 1


def center_gram_kernel(place_ref, e_ref, a_ref, b_ref, c_ref, d_ref, cent_ref, out_ref):
    total = BLOCKS * GROUP
    scale = 1.0 / math.sqrt(total)
    parts = (a_ref, b_ref, c_ref, d_ref)
    column_sum = None
    for part in parts:
        piece = jnp.sum(part[...].astype(jnp.float32), axis=0, keepdims=True)
        column_sum = piece if column_sum is None else column_sum + piece
    mean = column_sum / total
    for number, part in enumerate(parts):
        start = pl.multiple_of(place_ref[number] * GROUP, GROUP)
        cent_ref[pl.ds(start, GROUP), :] = (
            (part[...].astype(jnp.float32) - mean) * scale
        ).astype(jnp.bfloat16)
    for core, strips in enumerate(STRIPS):

        @pl.when(place_ref[4] == core)
        def _():
            at = 0
            for r, c, wide in strips:
                strip = lax.dot_general(
                    cent_ref[GROUP * r : GROUP * r + GROUP, :],
                    cent_ref[GROUP * c : GROUP * (c + wide), :],
                    (((1,), (1,)), ((), ())),
                    preferred_element_type=jnp.float32,
                )
                for n in range(wide):
                    out_ref[at : at + GROUP, :] = strip[:, GROUP * n : GROUP * n + GROUP]
                    at += GROUP

    column = lax.broadcasted_iota(jnp.int32, (GROUP, GROUP), 1)
    mine = (column // (GROUP // 2) == place_ref[5]) & (place_ref[6] == 0)
    out_ref[GROUP * (HELD - 1) :, :] = jnp.where(mine, e_ref[...], 0.0)


def lane(value, index):
    return jnp.broadcast_to(value[:, index : index + 1], (ROWS, GROUP))


def row(value, index):
    return jnp.broadcast_to(value[index : index + 1, :], (ROWS, GROUP))


def factor_block(rows):
    rows = list(rows)
    column = lax.broadcasted_iota(jnp.int32, (ROWS, GROUP), 1)
    line = lax.broadcasted_iota(jnp.int32, (ROWS, GROUP), 0)
    size = WIDE * ROWS
    inverse, recips = [], []
    for p in range(0, PANELS, WIDE):
        first = ROWS * p
        after = list(range(p + WIDE, min(p + 2 * WIDE, PANELS)))
        beyond = list(range(p + 2 * WIDE, PANELS))
        own = (column >= first) & (column < first + size)
        held = {
            (m, t): lane(rows[p + t], first + m) for m in range(size) for t in range(m // ROWS, WIDE)
        }
        next_held = {(m, i): lane(rows[i], first + m) for m in range(size) for i in after}
        work = [
            jnp.where(own, (column - first - ROWS * t == line).astype(jnp.float32), rows[p + t])
            for t in range(WIDE)
        ]
        following = {i: jnp.where(own, 0.0, rows[i]) for i in after}
        scale = [None] * WIDE
        for j in range(size):
            home, at = divmod(j, ROWS)
            pivot_row = row(work[home], at)
            spread = {m: row(held[j, m // ROWS], m % ROWS) for m in range(j, size)}
            recip = 1.0 / spread[j]
            scale[home] = recip if at == 0 else jnp.where(line == at, recip, scale[home])
            factor = {t: held[j, t] * recip for t in range(home, WIDE)}
            for m in range(j + 1, size):
                for t in range(m // ROWS, WIDE):
                    if m == j + 1:
                        held[m, t] = held[m, t] - (held[j, t] * spread[m]) * recip
                    else:
                        held[m, t] = held[m, t] - factor[t] * spread[m]
            for t in range(home, WIDE):
                part = jnp.where(line > at, factor[t], 0.0) if t == home else factor[t]
                work[t] = work[t] - part * pivot_row
            for i in after:
                part = next_held[j, i] * recip
                for m in range(j + 1, size):
                    next_held[m, i] = next_held[m, i] - part * spread[m]
                following[i] = following[i] - part * pivot_row
        for t in range(WIDE):
            inverse.append(jnp.where(column < first + size, work[t], 0.0))
            recips.append(scale[t])
        for i in after:
            rows[i] = following[i]
        if beyond:
            panel = jnp.concatenate(work, axis=0)
            scaled = jnp.concatenate([work[t] * scale[t] for t in range(WIDE)], axis=0)
            change = contract(stack_left(scaled, 0), stack_right(panel, 0), 0)
            for i in beyond:
                change_tile = change[ROWS * i : ROWS * i + ROWS, :]
                rows[i] = jnp.where(own, 0.0, rows[i]) - change_tile
    return inverse, recips


def split(value):
    high = value.astype(jnp.bfloat16)
    rest = value - high.astype(jnp.float32)
    middle = rest.astype(jnp.bfloat16)
    return high, middle, (rest - middle.astype(jnp.float32)).astype(jnp.bfloat16)


def stack_left(value, axis):
    high, middle, low = split(value)
    return jnp.concatenate([high, high, middle, middle, high, low], axis=axis)


def stack_right(value, axis):
    high, middle, low = split(value)
    return jnp.concatenate([high, middle, high, middle, low, high], axis=axis)


def contract(left, right, axis):
    return lax.dot_general(
        left, right, (((axis,), (0,)), ((), ())), preferred_element_type=jnp.float32
    )


def solve_kernel(place_ref, parts_ref, cent_ref, coeff_ref, update_ref, gram, low, rec, z):
    blocks = BLOCKS
    tiles = parts_ref.shape[1] // (2 * ROWS)

    def tile(core, block, p):
        number = PANELS * block + p
        start = ROWS * (core * tiles + number % tiles)
        return parts_ref[number // tiles, start : start + ROWS, :]

    for core, held in enumerate(LISTS):
        for n, (r, c) in enumerate(held):
            for p in range(PANELS):
                gram[r, c, ROWS * p : ROWS * p + ROWS, :] = tile(core, n, p)
    energy_sum = jnp.zeros((ROWS, GROUP), jnp.float32)
    for core in range(2):
        for high in range(2):
            for p in range(PANELS):
                value = lane(tile(core, HELD - 1, p), high * GROUP // 2)
                gram[2 * high + core, blocks, ROWS * p : ROWS * p + ROWS, :] = value
                energy_sum = energy_sum + value
    energy_mean = jnp.sum(energy_sum, axis=0, keepdims=True) / (blocks * GROUP)
    scale = 1.0 / math.sqrt(blocks * GROUP)
    for k in range(blocks):
        gram[k, blocks] = (gram[k, blocks] - energy_mean) * scale
    column = lax.broadcasted_iota(jnp.int32, (ROWS, GROUP), 1)
    line = lax.broadcasted_iota(jnp.int32, (ROWS, GROUP), 0)

    def step(k):
        panels = []
        for p in range(PANELS):
            ridge = jnp.where(column - ROWS * p == line, RIDGE, 0.0)
            panels.append(gram[k, k, ROWS * p : ROWS * p + ROWS, :] + ridge)
        inverse, recips = factor_block(panels)
        for p in range(PANELS):
            low[k, ROWS * p : ROWS * p + ROWS, :] = inverse[p]
            rec[k, ROWS * p : ROWS * p + ROWS, :] = recips[p]
        tri = stack_left(low[k], 1)
        later = range(k + 1, blocks + 1)
        ys = {j: contract(tri, stack_right(gram[k, j], 0), 1) for j in later}
        zs = {j: ys[j] * rec[k] for j in later}
        for j in later:
            z[k, j] = zs[j]
        right = {j: stack_right(zs[j], 0) for j in later}
        for i in range(k + 1, blocks):
            left = stack_left(ys[i], 0)
            for j in range(i, blocks + 1):
                gram[i, j] = gram[i, j] - contract(left, right[j], 0)

    for k in range(blocks):
        step(k)
    xs = [None] * blocks
    spread = [None] * blocks
    for k in range(blocks - 1, -1, -1):
        right = z[k, blocks]
        for j in range(k + 1, blocks):
            right = right - contract(stack_left(z[k, j], 1), spread[j], 1)
        xs[k] = contract(stack_left(low[k], 0), stack_right(right, 0), 0)
        spread[k] = stack_right(xs[k], 0)
        coeff_ref[GROUP * k : GROUP * k + GROUP, :] = xs[k]
    width = cent_ref.shape[1]
    for piece in range(width // GROUP):
        total = jnp.zeros((ROWS, GROUP), jnp.float32)
        for k in range(blocks):
            values = cent_ref[
                GROUP * k : GROUP * k + GROUP, GROUP * piece : GROUP * piece + GROUP
            ].astype(jnp.float32)
            scaled = values * xs[k]
            total = total + jnp.sum(scaled.reshape(PANELS, ROWS, GROUP), axis=0)
        update_ref[:, GROUP * piece : GROUP * piece + GROUP] = jnp.sum(
            total, axis=0, keepdims=True
        )


VMEM = pl.BlockSpec(memory_space=pltpu.VMEM)
SMEM = pl.BlockSpec(memory_space=pltpu.SMEM)


def center_gram(place, energies, parts):
    columns = parts[0].shape[1]
    return pl.pallas_call(
        center_gram_kernel,
        out_shape=(
            jax.ShapeDtypeStruct((BLOCKS * GROUP, columns), jnp.bfloat16),
            jax.ShapeDtypeStruct((HELD * GROUP, GROUP), jnp.float32),
        ),
        in_specs=[SMEM] + [VMEM] * 5,
        out_specs=(VMEM, VMEM),
        compiler_params=pltpu.CompilerParams(vmem_limit_bytes=32 * 1024 * 1024),
        name="center_gram",
    )(place, energies, *parts)


def solve(place, parts, cent):
    return pl.pallas_call(
        solve_kernel,
        out_shape=(
            jax.ShapeDtypeStruct((BLOCKS * GROUP, GROUP), jnp.float32),
            jax.ShapeDtypeStruct((1, cent.shape[1]), jnp.float32),
        ),
        in_specs=[SMEM] + [VMEM] * 2,
        out_specs=(VMEM, VMEM),
        scratch_shapes=[
            pltpu.VMEM((4, 5, GROUP, GROUP), jnp.float32),
            pltpu.VMEM((4, GROUP, GROUP), jnp.float32),
            pltpu.VMEM((4, GROUP, GROUP), jnp.float32),
            pltpu.VMEM((4, 5, GROUP, GROUP), jnp.float32),
        ],
        compiler_params=pltpu.CompilerParams(vmem_limit_bytes=32 * 1024 * 1024),
        name="solve",
    )(place, parts, cent)


SWAP = [(0, 1), (1, 0)]


def per_device(jacobian, energies):
    high = lax.axis_index("high")
    core = lax.axis_index("core")
    half = jacobian.shape[1] // 2
    keep = lax.dynamic_slice_in_dim(jacobian, high * half, half, 1)
    send = lax.dynamic_slice_in_dim(jacobian, (1 - high) * half, half, 1)
    far = lax.ppermute(send, "high", SWAP)
    near = lax.ppermute(keep, "core", SWAP)
    diagonal = lax.ppermute(far, "core", SWAP)
    place = jnp.stack(
        [
            2 * high + core,
            2 * (1 - high) + core,
            2 * high + 1 - core,
            2 * (1 - high) + 1 - core,
            core,
            high,
            lax.axis_index(("z", "x", "low")),
        ]
    ).astype(jnp.int32)
    spread = jnp.broadcast_to(energies[:, None], (GROUP, GROUP))
    cent, partial = center_gram(place, spread, (keep, far, near, diagonal))
    plane = ("high", "x", "low")
    peers = lax.axis_size(plane)
    parts = lax.all_to_all(
        partial.reshape(peers, -1, GROUP), plane, split_axis=0, concat_axis=0, tiled=True
    )
    chunk = jnp.sum(parts, axis=0)
    ring = lax.axis_size("z")
    one, two, three = (
        lax.ppermute(chunk, "z", [(n, (n + step) % ring) for n in range(ring)])
        for step in range(1, ring)
    )
    chunk = (chunk + two) + (one + three)
    other = lax.ppermute(chunk, "core", SWAP)
    pair = jnp.concatenate(
        [jnp.where(core == 0, chunk, other), jnp.where(core == 0, other, chunk)], axis=0
    )
    blocks = lax.all_to_all(
        jnp.broadcast_to(pair[None], (peers, *pair.shape)),
        plane,
        split_axis=0,
        concat_axis=0,
        tiled=True,
    )
    coeffs, update = solve(place, blocks, cent)
    own = lax.dynamic_slice_in_dim(coeffs, (2 * high + core) * GROUP, GROUP, 0)[:, 0]
    update = update[0] * math.sqrt(2 * half * lax.axis_size(("z", "x", "low")))
    away = lax.ppermute(update, "high", SWAP)
    lower = jnp.where(high == 0, update, away)
    upper = jnp.where(high == 0, away, update)
    return jnp.concatenate([lower, upper]), own


def solution(mesh):
    fine = Mesh(mesh.devices.reshape(2, 2, 4, 4, 2), ("high", "core", "z", "x", "low"))
    samples, params = ("high", "core"), ("z", "x", "low")
    return jax.shard_map(
        per_device,
        mesh=fine,
        in_specs=(P(samples, params), P(samples)),
        out_specs=(P(params), P(samples)),
        check_vma=False,
    )
```

```python
import math

import jax
import jax.numpy as jnp
from jax import lax
from jax.experimental import pallas as pl
from jax.experimental.pallas import tpu as pltpu
from jax.sharding import Mesh, PartitionSpec as P

GROUP = 128
ROWS = 8
WIDE = 2
PANELS = GROUP // ROWS
RIDGE = 0.05


BLOCKS = 4
STRIPS = (((0, 0, 4), (1, 1, 1)), ((1, 2, 2), (2, 2, 2), (3, 3, 1)))
LISTS = tuple(tuple((r, c + n) for r, c, w in strips for n in range(w)) for strips in STRIPS)
HELD = len(LISTS[0])
SPARE, SPAN = GROUP // 2, 16


def center_gram_kernel(place_ref, e_ref, a_ref, b_ref, c_ref, d_ref, cent_ref, out_ref):
    total = BLOCKS * GROUP
    scale = 1.0 / math.sqrt(total)
    parts = (a_ref, b_ref, c_ref, d_ref)
    column_sum = None
    for part in parts:
        piece = jnp.sum(part[...].astype(jnp.float32), axis=0, keepdims=True)
        column_sum = piece if column_sum is None else column_sum + piece
    mean = column_sum / total
    for number, part in enumerate(parts):
        start = pl.multiple_of(place_ref[number] * GROUP, GROUP)
        cent_ref[pl.ds(start, GROUP), :] = (
            (part[...].astype(jnp.float32) - mean) * scale
        ).astype(jnp.bfloat16)
    for core, strips in enumerate(STRIPS):

        @pl.when(place_ref[4] == core)
        def _():
            at = 0
            for r, c, wide in strips:
                strip = lax.dot_general(
                    cent_ref[GROUP * r : GROUP * r + GROUP, :],
                    cent_ref[GROUP * c : GROUP * (c + wide), :],
                    (((1,), (1,)), ((), ())),
                    preferred_element_type=jnp.float32,
                )
                for n in range(wide):
                    out_ref[at : at + GROUP, :] = strip[:, GROUP * n : GROUP * n + GROUP]
                    at += GROUP

            column = lax.broadcasted_iota(jnp.int32, (SPARE, GROUP), 1)
            pair = jnp.where(column < SPAN, e_ref[:SPARE, :], e_ref[SPARE:, :])
            diagonals = [n for n, (r, c) in enumerate(LISTS[core]) if r == c]
            for high, n in enumerate(diagonals):
                mine = (place_ref[5] == high) & (place_ref[6] == 0)
                rows = slice(GROUP * n + SPARE, GROUP * (n + 1))
                out_ref[rows, :] = jnp.where(
                    column < 2 * SPAN, jnp.where(mine, pair, 0.0), out_ref[rows, :]
                )


def lane(value, index):
    return jnp.broadcast_to(value[:, index : index + 1], (ROWS, GROUP))


def row(value, index):
    return jnp.broadcast_to(value[index : index + 1, :], (ROWS, GROUP))


def factor_block(rows):
    rows = list(rows)
    column = lax.broadcasted_iota(jnp.int32, (ROWS, GROUP), 1)
    line = lax.broadcasted_iota(jnp.int32, (ROWS, GROUP), 0)
    size = WIDE * ROWS
    inverse, recips = [], []
    for p in range(0, PANELS, WIDE):
        first = ROWS * p
        after = list(range(p + WIDE, min(p + 2 * WIDE, PANELS)))
        beyond = list(range(p + 2 * WIDE, PANELS))
        own = (column >= first) & (column < first + size)
        held = {
            (m, t): lane(rows[p + t], first + m) for m in range(size) for t in range(m // ROWS, WIDE)
        }
        next_held = {(m, i): lane(rows[i], first + m) for m in range(size) for i in after}
        work = [
            jnp.where(own, (column - first - ROWS * t == line).astype(jnp.float32), rows[p + t])
            for t in range(WIDE)
        ]
        following = {i: jnp.where(own, 0.0, rows[i]) for i in after}
        scale = [None] * WIDE
        for j in range(size):
            home, at = divmod(j, ROWS)
            pivot_row = row(work[home], at)
            spread = {m: row(held[j, m // ROWS], m % ROWS) for m in range(j, size)}
            recip = 1.0 / spread[j]
            scale[home] = recip if at == 0 else jnp.where(line == at, recip, scale[home])
            factor = {t: held[j, t] * recip for t in range(home, WIDE)}
            for m in range(j + 1, size):
                for t in range(m // ROWS, WIDE):
                    if m == j + 1:
                        held[m, t] = held[m, t] - (held[j, t] * spread[m]) * recip
                    else:
                        held[m, t] = held[m, t] - factor[t] * spread[m]
            for t in range(home, WIDE):
                part = jnp.where(line > at, factor[t], 0.0) if t == home else factor[t]
                work[t] = work[t] - part * pivot_row
            for i in after:
                part = next_held[j, i] * recip
                for m in range(j + 1, size):
                    next_held[m, i] = next_held[m, i] - part * spread[m]
                following[i] = following[i] - part * pivot_row
        for t in range(WIDE):
            inverse.append(jnp.where(column < first + size, work[t], 0.0))
            recips.append(scale[t])
        for i in after:
            rows[i] = following[i]
        if beyond:
            panel = jnp.concatenate(work, axis=0)
            scaled = jnp.concatenate([work[t] * scale[t] for t in range(WIDE)], axis=0)
            change = contract(stack_left(scaled, 0), stack_right(panel, 0), 0)
            for i in beyond:
                change_tile = change[ROWS * i : ROWS * i + ROWS, :]
                rows[i] = jnp.where(own, 0.0, rows[i]) - change_tile
    return inverse, recips


def split(value):
    high = value.astype(jnp.bfloat16)
    rest = value - high.astype(jnp.float32)
    middle = rest.astype(jnp.bfloat16)
    return high, middle, (rest - middle.astype(jnp.float32)).astype(jnp.bfloat16)


def stack_left(value, axis):
    high, middle, low = split(value)
    return jnp.concatenate([high, high, middle, middle, high, low], axis=axis)


def stack_right(value, axis):
    high, middle, low = split(value)
    return jnp.concatenate([high, middle, high, middle, low, high], axis=axis)


def contract(left, right, axis):
    return lax.dot_general(
        left, right, (((axis,), (0,)), ((), ())), preferred_element_type=jnp.float32
    )


def solve_kernel(
    place_ref, mine_ref, other_ref, cent_ref, coeff_ref, update_ref, gram, low, rec, z
):
    blocks = BLOCKS
    for core, held in enumerate(LISTS):
        for mine, ref in ((core, mine_ref), (1 - core, other_ref)):

            @pl.when(place_ref[4] == mine)
            def _():
                for n, (r, c) in enumerate(held):
                    gram[r, c] = ref[GROUP * n : GROUP * n + GROUP, :]

    energy_sum = jnp.zeros((ROWS, GROUP), jnp.float32)
    for core, held in enumerate(LISTS):
        for high, k in enumerate(r for r, c in held if r == c):
            for p in range(PANELS):
                which, start = divmod(ROWS * p, SPARE)
                tile = gram[k, k, SPARE + start : SPARE + start + ROWS, :]
                value = lane(tile, SPAN * which)
                gram[2 * high + core, blocks, ROWS * p : ROWS * p + ROWS, :] = value
                energy_sum = energy_sum + value
    energy_mean = jnp.sum(energy_sum, axis=0, keepdims=True) / (blocks * GROUP)
    scale = 1.0 / math.sqrt(blocks * GROUP)
    for k in range(blocks):
        gram[k, blocks] = (gram[k, blocks] - energy_mean) * scale
    column = lax.broadcasted_iota(jnp.int32, (ROWS, GROUP), 1)
    line = lax.broadcasted_iota(jnp.int32, (ROWS, GROUP), 0)

    def step(k):
        panels = []
        for p in range(PANELS):
            ridge = jnp.where(column - ROWS * p == line, RIDGE, 0.0)
            panels.append(gram[k, k, ROWS * p : ROWS * p + ROWS, :] + ridge)
        inverse, recips = factor_block(panels)
        for p in range(PANELS):
            low[k, ROWS * p : ROWS * p + ROWS, :] = inverse[p]
            rec[k, ROWS * p : ROWS * p + ROWS, :] = recips[p]
        tri = stack_left(low[k], 1)
        later = range(k + 1, blocks + 1)
        ys = {j: contract(tri, stack_right(gram[k, j], 0), 1) for j in later}
        zs = {j: ys[j] * rec[k] for j in later}
        for j in later:
            z[k, j] = zs[j]
        right = {j: stack_right(zs[j], 0) for j in later}
        for i in range(k + 1, blocks):
            left = stack_left(ys[i], 0)
            for j in range(i, blocks + 1):
                gram[i, j] = gram[i, j] - contract(left, right[j], 0)

    for k in range(blocks):
        step(k)
    xs = [None] * blocks
    spread = [None] * blocks
    for k in range(blocks - 1, -1, -1):
        right = z[k, blocks]
        for j in range(k + 1, blocks):
            right = right - contract(stack_left(z[k, j], 1), spread[j], 1)
        xs[k] = contract(stack_left(low[k], 0), stack_right(right, 0), 0)
        spread[k] = stack_right(xs[k], 0)
        coeff_ref[GROUP * k : GROUP * k + GROUP, :] = xs[k]
    width = cent_ref.shape[1]
    for piece in range(width // GROUP):
        total = jnp.zeros((ROWS, GROUP), jnp.float32)
        for k in range(blocks):
            values = cent_ref[
                GROUP * k : GROUP * k + GROUP, GROUP * piece : GROUP * piece + GROUP
            ].astype(jnp.float32)
            scaled = values * xs[k]
            total = total + jnp.sum(scaled.reshape(PANELS, ROWS, GROUP), axis=0)
        update_ref[:, GROUP * piece : GROUP * piece + GROUP] = jnp.sum(
            total, axis=0, keepdims=True
        )


VMEM = pl.BlockSpec(memory_space=pltpu.VMEM)
SMEM = pl.BlockSpec(memory_space=pltpu.SMEM)


def center_gram(place, energies, parts):
    columns = parts[0].shape[1]
    return pl.pallas_call(
        center_gram_kernel,
        out_shape=(
            jax.ShapeDtypeStruct((BLOCKS * GROUP, columns), jnp.bfloat16),
            jax.ShapeDtypeStruct((HELD * GROUP, GROUP), jnp.float32),
        ),
        in_specs=[SMEM] + [VMEM] * 5,
        out_specs=(VMEM, VMEM),
        compiler_params=pltpu.CompilerParams(vmem_limit_bytes=32 * 1024 * 1024),
        name="center_gram",
    )(place, energies, *parts)


def solve(place, mine, other, cent):
    return pl.pallas_call(
        solve_kernel,
        out_shape=(
            jax.ShapeDtypeStruct((BLOCKS * GROUP, GROUP), jnp.float32),
            jax.ShapeDtypeStruct((1, cent.shape[1]), jnp.float32),
        ),
        in_specs=[SMEM] + [VMEM] * 3,
        out_specs=(VMEM, VMEM),
        scratch_shapes=[
            pltpu.VMEM((4, 5, GROUP, GROUP), jnp.float32),
            pltpu.VMEM((4, GROUP, GROUP), jnp.float32),
            pltpu.VMEM((4, GROUP, GROUP), jnp.float32),
            pltpu.VMEM((4, 5, GROUP, GROUP), jnp.float32),
        ],
        compiler_params=pltpu.CompilerParams(vmem_limit_bytes=32 * 1024 * 1024),
        name="solve",
    )(place, mine, other, cent)


SWAP = [(0, 1), (1, 0)]


def per_device(jacobian, energies):
    high = lax.axis_index("high")
    core = lax.axis_index("core")
    half = jacobian.shape[1] // 2
    send = lax.dynamic_slice_in_dim(jacobian, (1 - high) * half, half, 1)
    send, jacobian = lax.optimization_barrier((send, jacobian))
    keep = lax.dynamic_slice_in_dim(jacobian, high * half, half, 1)
    far = lax.ppermute(send, "high", SWAP)
    near = lax.ppermute(keep, "core", SWAP)
    diagonal = lax.ppermute(far, "core", SWAP)
    place = jnp.stack(
        [
            2 * high + core,
            2 * (1 - high) + core,
            2 * high + 1 - core,
            2 * (1 - high) + 1 - core,
            core,
            high,
            lax.axis_index(("z", "x", "low")),
        ]
    ).astype(jnp.int32)
    spread = jnp.broadcast_to(energies[:, None], (GROUP, GROUP))
    cent, partial = center_gram(place, spread, (keep, far, near, diagonal))
    plane = ("high", "x", "low")
    peers = lax.axis_size(plane)
    parts = lax.all_to_all(
        partial.reshape(peers, -1, GROUP), plane, split_axis=0, concat_axis=0, tiled=True
    )
    chunk = jnp.sum(parts, axis=0)
    ring = lax.axis_size("z")
    one, two, three = (
        lax.ppermute(chunk, "z", [(n, (n + step) % ring) for n in range(ring)])
        for step in range(1, ring)
    )
    chunk = (chunk + two) + (one + three)
    mine = lax.all_to_all(
        jnp.broadcast_to(chunk[None], (peers, *chunk.shape)),
        plane,
        split_axis=0,
        concat_axis=0,
        tiled=True,
    ).reshape(HELD * GROUP, GROUP)
    other = lax.ppermute(mine, "core", SWAP)
    coeffs, update = solve(place, mine, other, cent)
    own = lax.dynamic_slice_in_dim(coeffs, (2 * high + core) * GROUP, GROUP, 0)[:, 0]
    update = update[0] * math.sqrt(2 * half * lax.axis_size(("z", "x", "low")))
    away = lax.ppermute(update, "high", SWAP)
    lower = jnp.where(high == 0, update, away)
    upper = jnp.where(high == 0, away, update)
    return jnp.concatenate([lower, upper]), own


def solution(mesh):
    fine = Mesh(mesh.devices.reshape(2, 2, 4, 4, 2), ("high", "core", "z", "x", "low"))
    samples, params = ("high", "core"), ("z", "x", "low")
    return jax.shard_map(
        per_device,
        mesh=fine,
        in_specs=(P(samples, params), P(samples)),
        out_specs=(P(params), P(samples)),
        check_vma=False,
    )
```

```python
import math

import jax
import jax.numpy as jnp
from jax import lax
from jax.experimental import pallas as pl
from jax.experimental.pallas import tpu as pltpu
from jax.sharding import Mesh, PartitionSpec as P

GROUP = 128
ROWS = 8
WIDE = 2
PANELS = GROUP // ROWS
RIDGE = 0.05


BLOCKS = 4
STRIPS = (((0, 0, 4), (1, 1, 1)), ((1, 2, 2), (2, 2, 2), (3, 3, 1)))
LISTS = tuple(tuple((r, c + n) for r, c, w in strips for n in range(w)) for strips in STRIPS)
HELD = len(LISTS[0])
SPARE, SPAN = GROUP // 2, 16


def center_gram_kernel(place_ref, e_ref, a_ref, b_ref, c_ref, d_ref, cent_ref, out_ref):
    total = BLOCKS * GROUP
    scale = 1.0 / math.sqrt(total)
    parts = (a_ref, b_ref, c_ref, d_ref)
    column_sum = None
    for part in parts:
        piece = jnp.sum(part[...].astype(jnp.float32), axis=0, keepdims=True)
        column_sum = piece if column_sum is None else column_sum + piece
    mean = column_sum / total
    for number, part in enumerate(parts):
        start = pl.multiple_of(place_ref[number] * GROUP, GROUP)
        cent_ref[pl.ds(start, GROUP), :] = (
            (part[...].astype(jnp.float32) - mean) * scale
        ).astype(jnp.bfloat16)
    for core, strips in enumerate(STRIPS):

        @pl.when(place_ref[4] == core)
        def _():
            at = 0
            for r, c, wide in strips:
                strip = lax.dot_general(
                    cent_ref[GROUP * r : GROUP * r + GROUP, :],
                    cent_ref[GROUP * c : GROUP * (c + wide), :],
                    (((1,), (1,)), ((), ())),
                    preferred_element_type=jnp.float32,
                )
                for n in range(wide):
                    out_ref[at : at + GROUP, :] = strip[:, GROUP * n : GROUP * n + GROUP]
                    at += GROUP

            column = lax.broadcasted_iota(jnp.int32, (SPARE, GROUP), 1)
            pair = jnp.where(column < SPAN, e_ref[:SPARE, :], e_ref[SPARE:, :])
            diagonals = [n for n, (r, c) in enumerate(LISTS[core]) if r == c]
            for high, n in enumerate(diagonals):
                mine = (place_ref[5] == high) & (place_ref[6] == 0)
                rows = slice(GROUP * n + SPARE, GROUP * (n + 1))
                out_ref[rows, :] = jnp.where(
                    column < 2 * SPAN, jnp.where(mine, pair, 0.0), out_ref[rows, :]
                )


def lane(value, index):
    return jnp.broadcast_to(value[:, index : index + 1], (ROWS, GROUP))


def row(value, index):
    return jnp.broadcast_to(value[index : index + 1, :], (ROWS, GROUP))


def factor_block(rows):
    rows = list(rows)
    column = lax.broadcasted_iota(jnp.int32, (ROWS, GROUP), 1)
    line = lax.broadcasted_iota(jnp.int32, (ROWS, GROUP), 0)
    size = WIDE * ROWS
    inverse, recips = [], []
    for p in range(0, PANELS, WIDE):
        first = ROWS * p
        after = list(range(p + WIDE, min(p + 2 * WIDE, PANELS)))
        beyond = list(range(p + 2 * WIDE, PANELS))
        own = (column >= first) & (column < first + size)
        held = {
            (m, t): lane(rows[p + t], first + m) for m in range(size) for t in range(m // ROWS, WIDE)
        }
        next_held = {(m, i): lane(rows[i], first + m) for m in range(size) for i in after}
        work = [
            jnp.where(own, (column - first - ROWS * t == line).astype(jnp.float32), rows[p + t])
            for t in range(WIDE)
        ]
        following = {i: jnp.where(own, 0.0, rows[i]) for i in after}
        scale = [None] * WIDE
        for j in range(size):
            home, at = divmod(j, ROWS)
            pivot_row = row(work[home], at)
            spread = {m: row(held[j, m // ROWS], m % ROWS) for m in range(j, size)}
            recip = 1.0 / spread[j]
            scale[home] = recip if at == 0 else jnp.where(line == at, recip, scale[home])
            factor = {t: held[j, t] * recip for t in range(home, WIDE)}
            for m in range(j + 1, size):
                for t in range(m // ROWS, WIDE):
                    held[m, t] = held[m, t] - factor[t] * spread[m]
            for t in range(home, WIDE):
                part = jnp.where(line > at, factor[t], 0.0) if t == home else factor[t]
                work[t] = work[t] - part * pivot_row
            for i in after:
                part = next_held[j, i] * recip
                for m in range(j + 1, size):
                    next_held[m, i] = next_held[m, i] - part * spread[m]
                following[i] = following[i] - part * pivot_row
        for t in range(WIDE):
            inverse.append(jnp.where(column < first + size, work[t], 0.0))
            recips.append(scale[t])
        for i in after:
            rows[i] = following[i]
        if beyond:
            panel = jnp.concatenate(work, axis=0)
            scaled = jnp.concatenate([work[t] * scale[t] for t in range(WIDE)], axis=0)
            change = contract(stack_left(scaled, 0), stack_right(panel, 0), 0)
            for i in beyond:
                change_tile = change[ROWS * i : ROWS * i + ROWS, :]
                rows[i] = jnp.where(own, 0.0, rows[i]) - change_tile
    return inverse, recips


def split(value):
    high = value.astype(jnp.bfloat16)
    rest = value - high.astype(jnp.float32)
    middle = rest.astype(jnp.bfloat16)
    return high, middle, (rest - middle.astype(jnp.float32)).astype(jnp.bfloat16)


def stack_left(value, axis):
    high, middle, low = split(value)
    return jnp.concatenate([high, high, middle, middle, high, low], axis=axis)


def stack_right(value, axis):
    high, middle, low = split(value)
    return jnp.concatenate([high, middle, high, middle, low, high], axis=axis)


def contract(left, right, axis):
    return lax.dot_general(
        left, right, (((axis,), (0,)), ((), ())), preferred_element_type=jnp.float32
    )


def solve_kernel(
    place_ref, mine_ref, other_ref, cent_ref, coeff_ref, update_ref, gram, rest
):
    blocks = BLOCKS
    for core, held in enumerate(LISTS):
        for mine, ref in ((core, mine_ref), (1 - core, other_ref)):

            @pl.when(place_ref[4] == mine)
            def _():
                for n, (r, c) in enumerate(held):
                    gram[r, :, GROUP * c : GROUP * c + GROUP] = ref[
                        GROUP * n : GROUP * n + GROUP, :
                    ]

    energy_sum = jnp.zeros((ROWS, GROUP), jnp.float32)
    for core, held in enumerate(LISTS):
        for high, k in enumerate(r for r, c in held if r == c):
            for p in range(PANELS):
                which, start = divmod(ROWS * p, SPARE)
                tile = gram[
                    k, SPARE + start : SPARE + start + ROWS, GROUP * k : GROUP * k + GROUP
                ]
                value = lane(tile, SPAN * which)
                gram[2 * high + core, ROWS * p : ROWS * p + ROWS, GROUP * blocks :] = value
                energy_sum = energy_sum + value
    energy_mean = jnp.sum(energy_sum, axis=0, keepdims=True) / (blocks * GROUP)
    scale = 1.0 / math.sqrt(blocks * GROUP)
    for k in range(blocks):
        gram[k, :, GROUP * blocks :] = (gram[k, :, GROUP * blocks :] - energy_mean) * scale
    column = lax.broadcasted_iota(jnp.int32, (ROWS, GROUP), 1)
    line = lax.broadcasted_iota(jnp.int32, (ROWS, GROUP), 0)

    def step(k):
        panels = []
        for p in range(PANELS):
            ridge = jnp.where(column - ROWS * p == line, RIDGE, 0.0)
            tile = gram[k, ROWS * p : ROWS * p + ROWS, GROUP * k : GROUP * k + GROUP]
            panels.append(tile + ridge)
        inverse, recips = factor_block(panels)
        triangle = jnp.concatenate(inverse, axis=0)
        tri = stack_left(triangle, 1)
        tri_turned = stack_left(triangle, 0)
        wide = slice(GROUP * (k + 1), GROUP * (blocks + 1))
        y = contract(tri, stack_right(gram[k, :, wide], 0), 1)
        inverse_d = jnp.concatenate(recips, axis=0)
        right = stack_right(y * jnp.concatenate([inverse_d] * (blocks - k), axis=1), 0)
        for i in range(k + 1, blocks):
            skip = GROUP * (i - k - 1)
            left = stack_left(y[:, skip : skip + GROUP], 0)
            place = slice(GROUP * i, GROUP * (blocks + 1))
            gram[i, :, place] = gram[i, :, place] - contract(left, right[:, skip:], 0)
        rest[k, :, wide] = contract(tri_turned, right, 0)
        if k:
            found = stack_right(rest[k, :, wide], 0)
        for i in range(k):
            left = stack_left(rest[i, :, GROUP * k : GROUP * k + GROUP], 1)
            rest[i, :, wide] = rest[i, :, wide] - contract(left, found, 1)

    for k in range(blocks):
        step(k)
    xs = [rest[k, :, GROUP * blocks :] for k in range(blocks)]
    for k in range(blocks):
        coeff_ref[GROUP * k : GROUP * k + GROUP, :] = xs[k]
    width = cent_ref.shape[1]
    for piece in range(width // GROUP):
        total = jnp.zeros((ROWS, GROUP), jnp.float32)
        for k in range(blocks):
            values = cent_ref[
                GROUP * k : GROUP * k + GROUP, GROUP * piece : GROUP * piece + GROUP
            ].astype(jnp.float32)
            scaled = values * xs[k]
            total = total + jnp.sum(scaled.reshape(PANELS, ROWS, GROUP), axis=0)
        update_ref[:, GROUP * piece : GROUP * piece + GROUP] = jnp.sum(
            total, axis=0, keepdims=True
        )


VMEM = pl.BlockSpec(memory_space=pltpu.VMEM)
SMEM = pl.BlockSpec(memory_space=pltpu.SMEM)


def center_gram(place, energies, parts):
    columns = parts[0].shape[1]
    return pl.pallas_call(
        center_gram_kernel,
        out_shape=(
            jax.ShapeDtypeStruct((BLOCKS * GROUP, columns), jnp.bfloat16),
            jax.ShapeDtypeStruct((HELD * GROUP, GROUP), jnp.float32),
        ),
        in_specs=[SMEM] + [VMEM] * 5,
        out_specs=(VMEM, VMEM),
        compiler_params=pltpu.CompilerParams(vmem_limit_bytes=32 * 1024 * 1024),
        name="center_gram",
    )(place, energies, *parts)


def solve(place, mine, other, cent):
    return pl.pallas_call(
        solve_kernel,
        out_shape=(
            jax.ShapeDtypeStruct((BLOCKS * GROUP, GROUP), jnp.float32),
            jax.ShapeDtypeStruct((1, cent.shape[1]), jnp.float32),
        ),
        in_specs=[SMEM] + [VMEM] * 3,
        out_specs=(VMEM, VMEM),
        scratch_shapes=[
            pltpu.VMEM((BLOCKS, GROUP, (BLOCKS + 1) * GROUP), jnp.float32),
            pltpu.VMEM((BLOCKS, GROUP, (BLOCKS + 1) * GROUP), jnp.float32),
        ],
        compiler_params=pltpu.CompilerParams(vmem_limit_bytes=32 * 1024 * 1024),
        name="solve",
    )(place, mine, other, cent)


SWAP = [(0, 1), (1, 0)]


def per_device(jacobian, energies):
    high = lax.axis_index("high")
    core = lax.axis_index("core")
    half = jacobian.shape[1] // 2
    send = lax.dynamic_slice_in_dim(jacobian, (1 - high) * half, half, 1)
    send, jacobian = lax.optimization_barrier((send, jacobian))
    keep = lax.dynamic_slice_in_dim(jacobian, high * half, half, 1)
    far = lax.ppermute(send, "high", SWAP)
    near = lax.ppermute(keep, "core", SWAP)
    diagonal = lax.ppermute(far, "core", SWAP)
    place = jnp.stack(
        [
            2 * high + core,
            2 * (1 - high) + core,
            2 * high + 1 - core,
            2 * (1 - high) + 1 - core,
            core,
            high,
            lax.axis_index(("z", "x", "low")),
        ]
    ).astype(jnp.int32)
    spread = jnp.broadcast_to(energies[:, None], (GROUP, GROUP))
    cent, partial = center_gram(place, spread, (keep, far, near, diagonal))
    plane = ("high", "x", "low")
    peers = lax.axis_size(plane)
    parts = lax.all_to_all(
        partial.reshape(peers, -1, GROUP), plane, split_axis=0, concat_axis=0, tiled=True
    )
    chunk = jnp.sum(parts, axis=0)
    ring = lax.axis_size("z")
    one, two, three = (
        lax.ppermute(chunk, "z", [(n, (n + step) % ring) for n in range(ring)])
        for step in range(1, ring)
    )
    chunk = (chunk + two) + (one + three)
    mine = lax.all_to_all(
        jnp.broadcast_to(chunk[None], (peers, *chunk.shape)),
        plane,
        split_axis=0,
        concat_axis=0,
        tiled=True,
    ).reshape(HELD * GROUP, GROUP)
    other = lax.ppermute(mine, "core", SWAP)
    coeffs, update = solve(place, mine, other, cent)
    own = lax.dynamic_slice_in_dim(coeffs, (2 * high + core) * GROUP, GROUP, 0)[:, 0]
    update = update[0] * math.sqrt(2 * half * lax.axis_size(("z", "x", "low")))
    away = lax.ppermute(update, "high", SWAP)
    lower = jnp.where(high == 0, update, away)
    upper = jnp.where(high == 0, away, update)
    return jnp.concatenate([lower, upper]), own


def solution(mesh):
    fine = Mesh(mesh.devices.reshape(2, 2, 4, 4, 2), ("high", "core", "z", "x", "low"))
    samples, params = ("high", "core"), ("z", "x", "low")
    return jax.shard_map(
        per_device,
        mesh=fine,
        in_specs=(P(samples, params), P(samples)),
        out_specs=(P(params), P(samples)),
        check_vma=False,
    )
```

```python
import math

import jax
import jax.numpy as jnp
from jax import lax
from jax.experimental import pallas as pl
from jax.experimental.pallas import tpu as pltpu
from jax.sharding import Mesh, PartitionSpec as P

GROUP = 128
ROWS = 8
WIDE = 2
PANELS = GROUP // ROWS
COPIES = 4
RIDGE = 0.05


BLOCKS = 4
STRIPS = (((0, 0, 4), (1, 1, 1)), ((1, 2, 2), (2, 2, 2), (3, 3, 1)))
LISTS = tuple(tuple((r, c + n) for r, c, w in strips for n in range(w)) for strips in STRIPS)
HELD = len(LISTS[0])
SPARE, SPAN = GROUP // 2, 16


def center_gram_kernel(place_ref, e_ref, a_ref, b_ref, c_ref, d_ref, cent_ref, out_ref):
    total = BLOCKS * GROUP
    scale = 1.0 / math.sqrt(total)
    parts = (a_ref, b_ref, c_ref, d_ref)
    column_sum = None
    for part in parts:
        piece = jnp.sum(part[...].astype(jnp.float32), axis=0, keepdims=True)
        column_sum = piece if column_sum is None else column_sum + piece
    mean = column_sum / total
    for number, part in enumerate(parts):
        start = pl.multiple_of(place_ref[number] * GROUP, GROUP)
        cent_ref[pl.ds(start, GROUP), :] = (
            (part[...].astype(jnp.float32) - mean) * scale
        ).astype(jnp.bfloat16)
    for core, strips in enumerate(STRIPS):

        @pl.when(place_ref[4] == core)
        def _():
            at = 0
            for r, c, wide in strips:
                strip = lax.dot_general(
                    cent_ref[GROUP * r : GROUP * r + GROUP, :],
                    cent_ref[GROUP * c : GROUP * (c + wide), :],
                    (((1,), (1,)), ((), ())),
                    preferred_element_type=jnp.float32,
                )
                for n in range(wide):
                    out_ref[at : at + GROUP, :] = strip[:, GROUP * n : GROUP * n + GROUP]
                    at += GROUP

            column = lax.broadcasted_iota(jnp.int32, (SPARE, GROUP), 1)
            pair = jnp.where(column < SPAN, e_ref[:SPARE, :], e_ref[SPARE:, :])
            diagonals = [n for n, (r, c) in enumerate(LISTS[core]) if r == c]
            for high, n in enumerate(diagonals):
                mine = (place_ref[5] == high) & (place_ref[6] == 0)
                rows = slice(GROUP * n + SPARE, GROUP * (n + 1))
                out_ref[rows, :] = jnp.where(
                    column < 2 * SPAN, jnp.where(mine, pair, 0.0), out_ref[rows, :]
                )


def lane(value, index):
    return jnp.broadcast_to(value[:, index : index + 1], (ROWS, GROUP))


def row(value, index):
    return jnp.broadcast_to(value[index : index + 1, :], (ROWS, GROUP))


def factor_block(rows):
    rows = list(rows)
    column = lax.broadcasted_iota(jnp.int32, (ROWS, GROUP), 1)
    line = lax.broadcasted_iota(jnp.int32, (ROWS, GROUP), 0)
    size = WIDE * ROWS
    inverse, recips = [], []
    for p in range(0, PANELS, WIDE):
        first = ROWS * p
        after = list(range(p + WIDE, min(p + 2 * WIDE, PANELS)))
        beyond = list(range(p + 2 * WIDE, PANELS))
        own = (column >= first) & (column < first + size)
        held = {
            (m, t): lane(rows[p + t], first + m) for m in range(size) for t in range(m // ROWS, WIDE)
        }
        next_held = {(m, i): lane(rows[i], first + m) for m in range(size) for i in after}
        work = [
            jnp.where(own, (column - first - ROWS * t == line).astype(jnp.float32), rows[p + t])
            for t in range(WIDE)
        ]
        following = {i: jnp.where(own, 0.0, rows[i]) for i in after}
        scale = [None] * WIDE
        for j in range(size):
            home, at = divmod(j, ROWS)
            pivot_row = row(work[home], at)
            spread = {m: row(held[j, m // ROWS], m % ROWS) for m in range(j, size)}
            recip = 1.0 / spread[j]
            scale[home] = recip if at == 0 else jnp.where(line == at, recip, scale[home])
            factor = {t: held[j, t] * recip for t in range(home, WIDE)}
            for m in range(j + 1, size):
                for t in range(m // ROWS, WIDE):
                    held[m, t] = held[m, t] - factor[t] * spread[m]
            for t in range(home, WIDE):
                part = jnp.where(line > at, factor[t], 0.0) if t == home else factor[t]
                work[t] = work[t] - part * pivot_row
            for i in after:
                part = next_held[j, i] * recip
                for m in range(j + 1, size):
                    next_held[m, i] = next_held[m, i] - part * spread[m]
                following[i] = following[i] - part * pivot_row
        for t in range(WIDE):
            inverse.append(jnp.where(column < first + size, work[t], 0.0))
            recips.append(scale[t])
        for i in after:
            rows[i] = following[i]
        if beyond:
            panel = jnp.concatenate(work, axis=0)
            scaled = jnp.concatenate([work[t] * scale[t] for t in range(WIDE)], axis=0)
            change = contract(stack_left(scaled, 0), stack_right(panel, 0), 0)
            for i in beyond:
                change_tile = change[ROWS * i : ROWS * i + ROWS, :]
                rows[i] = jnp.where(own, 0.0, rows[i]) - change_tile
    return inverse, recips


def split(value):
    high = value.astype(jnp.bfloat16)
    rest = value - high.astype(jnp.float32)
    middle = rest.astype(jnp.bfloat16)
    return high, middle, (rest - middle.astype(jnp.float32)).astype(jnp.bfloat16)


def stack_left(value, axis):
    high, middle, low = split(value)
    return jnp.concatenate([high, high, middle, middle, high, low], axis=axis)


def stack_right(value, axis):
    high, middle, low = split(value)
    return jnp.concatenate([high, middle, high, middle, low, high], axis=axis)


def contract(left, right, axis):
    return lax.dot_general(
        left, right, (((axis,), (0,)), ((), ())), preferred_element_type=jnp.float32
    )


def solve_kernel(
    place_ref, mine_ref, other_ref, cent_ref, coeff_ref, update_ref, gram, rest
):
    blocks = BLOCKS
    for core, held in enumerate(LISTS):
        for mine, ref in ((core, mine_ref), (1 - core, other_ref)):

            @pl.when(place_ref[4] == mine)
            def _():
                for n, (r, c) in enumerate(held):
                    gram[r, :, GROUP * c : GROUP * c + GROUP] = ref[
                        GROUP * n : GROUP * n + GROUP, :
                    ]

    energy_sum = jnp.zeros((ROWS, GROUP), jnp.float32)
    for core, held in enumerate(LISTS):
        for high, k in enumerate(r for r, c in held if r == c):
            for p in range(PANELS):
                which, start = divmod(ROWS * p, SPARE)
                tile = gram[
                    k, SPARE + start : SPARE + start + ROWS, GROUP * k : GROUP * k + GROUP
                ]
                value = lane(tile, SPAN * which)
                gram[2 * high + core, ROWS * p : ROWS * p + ROWS, GROUP * blocks :] = value
                energy_sum = energy_sum + value
    energy_mean = jnp.sum(energy_sum, axis=0, keepdims=True) / (blocks * GROUP)
    scale = 1.0 / math.sqrt(blocks * GROUP)
    for k in range(blocks):
        gram[k, :, GROUP * blocks :] = (gram[k, :, GROUP * blocks :] - energy_mean) * scale
    column = lax.broadcasted_iota(jnp.int32, (ROWS, GROUP), 1)
    line = lax.broadcasted_iota(jnp.int32, (ROWS, GROUP), 0)

    def step(k):
        panels = []
        for p in range(PANELS):
            ridge = jnp.where(column - ROWS * p == line, RIDGE, 0.0)
            tile = gram[k, ROWS * p : ROWS * p + ROWS, GROUP * k : GROUP * k + GROUP]
            panels.append(tile + ridge)
        inverse, recips = factor_block(panels)
        triangle = jnp.concatenate(inverse, axis=0)
        tri = stack_left(triangle, 1)
        tri_turned = stack_left(triangle, 0)
        wide = slice(GROUP * (k + 1), GROUP * (blocks + 1))
        y = contract(tri, stack_right(gram[k, :, wide], 0), 1)
        inverse_d = jnp.concatenate(recips, axis=0)
        right = stack_right(y * jnp.concatenate([inverse_d] * (blocks - k), axis=1), 0)
        for i in range(k + 1, blocks):
            skip = GROUP * (i - k - 1)
            left = stack_left(y[:, skip : skip + GROUP], 0)
            place = slice(GROUP * i, GROUP * (blocks + 1))
            gram[i, :, place] = gram[i, :, place] - contract(left, right[:, skip:], 0)
        rest[k, :, wide] = contract(tri_turned, right, 0)
        if k:
            found = stack_right(rest[k, :, wide], 0)
        for i in range(k):
            left = stack_left(rest[i, :, GROUP * k : GROUP * k + GROUP], 1)
            rest[i, :, wide] = rest[i, :, wide] - contract(left, found, 1)

    for k in range(blocks):
        step(k)
    xs = [rest[k, :, GROUP * blocks :] for k in range(blocks)]
    for k in range(blocks):
        coeff_ref[GROUP * k : GROUP * k + GROUP, :] = xs[k]
    width = cent_ref.shape[1]
    for piece in range(width // GROUP):
        total = jnp.zeros((ROWS, GROUP), jnp.float32)
        for k in range(blocks):
            values = cent_ref[
                GROUP * k : GROUP * k + GROUP, GROUP * piece : GROUP * piece + GROUP
            ].astype(jnp.float32)
            scaled = values * xs[k]
            total = total + jnp.sum(scaled.reshape(PANELS, ROWS, GROUP), axis=0)
        update_ref[:, GROUP * piece : GROUP * piece + GROUP] = jnp.sum(
            total, axis=0, keepdims=True
        )


def half_kernel(source_ref, half_ref, sems):
    columns = half_ref.shape[1]
    start = pl.multiple_of((1 - lax.axis_index("high")) * columns, columns)
    copies = []
    for n in range(COPIES):
        rows = pl.ds(n * (GROUP // COPIES), GROUP // COPIES)
        copies.append(
            pltpu.make_async_copy(
                source_ref.at[rows, pl.ds(start, columns)], half_ref.at[rows, :], sems.at[n]
            )
        )
    for copy in copies:
        copy.start()
    for copy in copies:
        copy.wait()


VMEM = pl.BlockSpec(memory_space=pltpu.VMEM)
SMEM = pl.BlockSpec(memory_space=pltpu.SMEM)


def other_half(jacobian):
    rows, columns = jacobian.shape
    return pl.pallas_call(
        half_kernel,
        out_shape=jax.ShapeDtypeStruct((rows, columns // 2), jacobian.dtype),
        in_specs=[pl.BlockSpec(memory_space=pl.ANY)],
        out_specs=pl.BlockSpec(memory_space=pl.ANY),
        scratch_shapes=[pltpu.SemaphoreType.DMA((COPIES,))],
        compiler_params=pltpu.CompilerParams(vmem_limit_bytes=60 * 1024 * 1024),
        name="other_half",
    )(jacobian)


def center_gram(place, energies, parts):
    columns = parts[0].shape[1]
    return pl.pallas_call(
        center_gram_kernel,
        out_shape=(
            jax.ShapeDtypeStruct((BLOCKS * GROUP, columns), jnp.bfloat16),
            jax.ShapeDtypeStruct((HELD * GROUP, GROUP), jnp.float32),
        ),
        in_specs=[SMEM] + [VMEM] * 5,
        out_specs=(VMEM, VMEM),
        compiler_params=pltpu.CompilerParams(vmem_limit_bytes=32 * 1024 * 1024),
        name="center_gram",
    )(place, energies, *parts)


def solve(place, mine, other, cent):
    return pl.pallas_call(
        solve_kernel,
        out_shape=(
            jax.ShapeDtypeStruct((BLOCKS * GROUP, GROUP), jnp.float32),
            jax.ShapeDtypeStruct((1, cent.shape[1]), jnp.float32),
        ),
        in_specs=[SMEM] + [VMEM] * 3,
        out_specs=(VMEM, VMEM),
        scratch_shapes=[
            pltpu.VMEM((BLOCKS, GROUP, (BLOCKS + 1) * GROUP), jnp.float32),
            pltpu.VMEM((BLOCKS, GROUP, (BLOCKS + 1) * GROUP), jnp.float32),
        ],
        compiler_params=pltpu.CompilerParams(vmem_limit_bytes=32 * 1024 * 1024),
        name="solve",
    )(place, mine, other, cent)


SWAP = [(0, 1), (1, 0)]


def per_device(jacobian, energies):
    high = lax.axis_index("high")
    core = lax.axis_index("core")
    half = jacobian.shape[1] // 2
    send = other_half(jacobian)
    keep = lax.dynamic_slice_in_dim(jacobian, high * half, half, 1)
    far = lax.ppermute(send, "high", SWAP)
    near = lax.ppermute(keep, "core", SWAP)
    diagonal = lax.ppermute(far, "core", SWAP)
    place = jnp.stack(
        [
            2 * high + core,
            2 * (1 - high) + core,
            2 * high + 1 - core,
            2 * (1 - high) + 1 - core,
            core,
            high,
            lax.axis_index(("z", "x", "low")),
        ]
    ).astype(jnp.int32)
    spread = jnp.broadcast_to(energies[:, None], (GROUP, GROUP))
    cent, partial = center_gram(place, spread, (keep, far, near, diagonal))
    plane = ("high", "x", "low")
    peers = lax.axis_size(plane)
    parts = lax.all_to_all(
        partial.reshape(peers, -1, GROUP), plane, split_axis=0, concat_axis=0, tiled=True
    )
    chunk = jnp.sum(parts, axis=0)
    ring = lax.axis_size("z")
    one, three, two = (
        lax.ppermute(chunk, "z", [(n, (n + step) % ring) for n in range(ring)])
        for step in (1, 3, 2)
    )
    chunk = (chunk + two) + (one + three)
    mine = lax.all_to_all(
        jnp.broadcast_to(chunk[None], (peers, *chunk.shape)),
        plane,
        split_axis=0,
        concat_axis=0,
        tiled=True,
    ).reshape(HELD * GROUP, GROUP)
    other = lax.ppermute(mine, "core", SWAP)
    coeffs, update = solve(place, mine, other, cent)
    own = lax.dynamic_slice_in_dim(coeffs, (2 * high + core) * GROUP, GROUP, 0)[:, 0]
    update = update[0] * math.sqrt(2 * half * lax.axis_size(("z", "x", "low")))
    away = lax.ppermute(update, "high", SWAP)
    lower = jnp.where(high == 0, update, away)
    upper = jnp.where(high == 0, away, update)
    return jnp.concatenate([lower, upper]), own


def solution(mesh):
    fine = Mesh(mesh.devices.reshape(2, 2, 4, 4, 2), ("high", "core", "z", "x", "low"))
    samples, params = ("high", "core"), ("z", "x", "low")
    return jax.shard_map(
        per_device,
        mesh=fine,
        in_specs=(P(samples, params), P(samples)),
        out_specs=(P(params), P(samples)),
        check_vma=False,
    )
```

```python
import math

import jax
import jax.numpy as jnp
from jax import lax
from jax.experimental import pallas as pl
from jax.experimental.pallas import tpu as pltpu
from jax.sharding import Mesh, PartitionSpec as P

GROUP = 128
ROWS = 8
WIDE = 2
PANELS = GROUP // ROWS
RIDGE = 0.05


BLOCKS = 4
STRIPS = (((0, 0, 4), (1, 1, 1)), ((1, 2, 2), (2, 2, 2), (3, 3, 1)))
LISTS = tuple(tuple((r, c + n) for r, c, w in strips for n in range(w)) for strips in STRIPS)
HELD = len(LISTS[0])
SPARE, SPAN = GROUP // 2, 16


def center_gram_kernel(place_ref, e_ref, a_ref, b_ref, c_ref, d_ref, cent_ref, out_ref):
    total = BLOCKS * GROUP
    scale = 1.0 / math.sqrt(total)
    parts = (a_ref, b_ref, c_ref, d_ref)
    column_sum = None
    for part in parts:
        piece = jnp.sum(part[...].astype(jnp.float32), axis=0, keepdims=True)
        column_sum = piece if column_sum is None else column_sum + piece
    mean = column_sum / total
    for number, part in enumerate(parts):
        start = pl.multiple_of(place_ref[number] * GROUP, GROUP)
        cent_ref[pl.ds(start, GROUP), :] = (
            (part[...].astype(jnp.float32) - mean) * scale
        ).astype(jnp.bfloat16)
    for core, strips in enumerate(STRIPS):

        @pl.when(place_ref[4] == core)
        def _():
            at = 0
            for r, c, wide in strips:
                strip = lax.dot_general(
                    cent_ref[GROUP * r : GROUP * r + GROUP, :],
                    cent_ref[GROUP * c : GROUP * (c + wide), :],
                    (((1,), (1,)), ((), ())),
                    preferred_element_type=jnp.float32,
                )
                for n in range(wide):
                    out_ref[at : at + GROUP, :] = strip[:, GROUP * n : GROUP * n + GROUP]
                    at += GROUP

            column = lax.broadcasted_iota(jnp.int32, (SPARE, GROUP), 1)
            pair = jnp.where(column < SPAN, e_ref[:SPARE, :], e_ref[SPARE:, :])
            diagonals = [n for n, (r, c) in enumerate(LISTS[core]) if r == c]
            for high, n in enumerate(diagonals):
                mine = (place_ref[5] == high) & (place_ref[6] == 0)
                rows = slice(GROUP * n + SPARE, GROUP * (n + 1))
                out_ref[rows, :] = jnp.where(
                    column < 2 * SPAN, jnp.where(mine, pair, 0.0), out_ref[rows, :]
                )


def lane(value, index):
    return jnp.broadcast_to(value[:, index : index + 1], (ROWS, GROUP))


def row(value, index):
    return jnp.broadcast_to(value[index : index + 1, :], (ROWS, GROUP))


def factor_block(rows):
    rows = list(rows)
    column = lax.broadcasted_iota(jnp.int32, (ROWS, GROUP), 1)
    line = lax.broadcasted_iota(jnp.int32, (ROWS, GROUP), 0)
    size = WIDE * ROWS
    inverse, recips = [], []
    for p in range(0, PANELS, WIDE):
        first = ROWS * p
        after = list(range(p + WIDE, min(p + 2 * WIDE, PANELS)))
        beyond = list(range(p + 2 * WIDE, PANELS))
        own = (column >= first) & (column < first + size)
        held = {
            (m, t): lane(rows[p + t], first + m) for m in range(size) for t in range(m // ROWS, WIDE)
        }
        next_held = {(m, i): lane(rows[i], first + m) for m in range(size) for i in after}
        work = [
            jnp.where(own, (column - first - ROWS * t == line).astype(jnp.float32), rows[p + t])
            for t in range(WIDE)
        ]
        following = {i: jnp.where(own, 0.0, rows[i]) for i in after}
        scale = [None] * WIDE
        for j in range(size):
            home, at = divmod(j, ROWS)
            pivot_row = row(work[home], at)
            spread = {m: row(held[j, m // ROWS], m % ROWS) for m in range(j, size)}
            recip = 1.0 / spread[j]
            scale[home] = recip if at == 0 else jnp.where(line == at, recip, scale[home])
            factor = {t: held[j, t] * recip for t in range(home, WIDE)}
            for m in range(j + 1, size):
                for t in range(m // ROWS, WIDE):
                    held[m, t] = held[m, t] - factor[t] * spread[m]
            for t in range(home, WIDE):
                part = jnp.where(line > at, factor[t], 0.0) if t == home else factor[t]
                work[t] = work[t] - part * pivot_row
            for i in after:
                part = next_held[j, i] * recip
                for m in range(j + 1, size):
                    next_held[m, i] = next_held[m, i] - part * spread[m]
                following[i] = following[i] - part * pivot_row
        for t in range(WIDE):
            inverse.append(jnp.where(column < first + size, work[t], 0.0))
            recips.append(scale[t])
        for i in after:
            rows[i] = following[i]
        if beyond:
            panel = jnp.concatenate(work, axis=0)
            scaled = jnp.concatenate([work[t] * scale[t] for t in range(WIDE)], axis=0)
            change = contract(stack_left(scaled, 0), stack_right(panel, 0), 0)
            for i in beyond:
                change_tile = change[ROWS * i : ROWS * i + ROWS, :]
                rows[i] = jnp.where(own, 0.0, rows[i]) - change_tile
    return inverse, recips


def split(value):
    high = value.astype(jnp.bfloat16)
    rest = value - high.astype(jnp.float32)
    middle = rest.astype(jnp.bfloat16)
    return high, middle, (rest - middle.astype(jnp.float32)).astype(jnp.bfloat16)


def stack_left(value, axis):
    high, middle, low = split(value)
    return jnp.concatenate([high, high, middle, middle, high, low], axis=axis)


def stack_right(value, axis):
    high, middle, low = split(value)
    return jnp.concatenate([high, middle, high, middle, low, high], axis=axis)


def contract(left, right, axis):
    return lax.dot_general(
        left, right, (((axis,), (0,)), ((), ())), preferred_element_type=jnp.float32
    )


def solve_kernel(parts_ref, cent_ref, coeff_ref, update_ref, gram, rest):
    blocks = BLOCKS
    for core, held in enumerate(LISTS):
        for n, (r, c) in enumerate(held):
            start = GROUP * (HELD * core + n)
            gram[r, :, GROUP * c : GROUP * c + GROUP] = parts_ref[start : start + GROUP, :]
    energy_sum = jnp.zeros((ROWS, GROUP), jnp.float32)
    for core, held in enumerate(LISTS):
        for high, k in enumerate(r for r, c in held if r == c):
            for p in range(PANELS):
                which, start = divmod(ROWS * p, SPARE)
                tile = gram[
                    k, SPARE + start : SPARE + start + ROWS, GROUP * k : GROUP * k + GROUP
                ]
                value = lane(tile, SPAN * which)
                gram[2 * high + core, ROWS * p : ROWS * p + ROWS, GROUP * blocks :] = value
                energy_sum = energy_sum + value
    energy_mean = jnp.sum(energy_sum, axis=0, keepdims=True) / (blocks * GROUP)
    scale = 1.0 / math.sqrt(blocks * GROUP)
    for k in range(blocks):
        gram[k, :, GROUP * blocks :] = (gram[k, :, GROUP * blocks :] - energy_mean) * scale
    column = lax.broadcasted_iota(jnp.int32, (ROWS, GROUP), 1)
    line = lax.broadcasted_iota(jnp.int32, (ROWS, GROUP), 0)

    def step(k):
        panels = []
        for p in range(PANELS):
            ridge = jnp.where(column - ROWS * p == line, RIDGE, 0.0)
            tile = gram[k, ROWS * p : ROWS * p + ROWS, GROUP * k : GROUP * k + GROUP]
            panels.append(tile + ridge)
        inverse, recips = factor_block(panels)
        triangle = jnp.concatenate(inverse, axis=0)
        tri = stack_left(triangle, 1)
        tri_turned = stack_left(triangle, 0)
        wide = slice(GROUP * (k + 1), GROUP * (blocks + 1))
        y = contract(tri, stack_right(gram[k, :, wide], 0), 1)
        inverse_d = jnp.concatenate(recips, axis=0)
        right = stack_right(y * jnp.concatenate([inverse_d] * (blocks - k), axis=1), 0)
        for i in range(k + 1, blocks):
            skip = GROUP * (i - k - 1)
            left = stack_left(y[:, skip : skip + GROUP], 0)
            place = slice(GROUP * i, GROUP * (blocks + 1))
            gram[i, :, place] = gram[i, :, place] - contract(left, right[:, skip:], 0)
        rest[k, :, wide] = contract(tri_turned, right, 0)
        if k:
            found = stack_right(rest[k, :, wide], 0)
        for i in range(k):
            left = stack_left(rest[i, :, GROUP * k : GROUP * k + GROUP], 1)
            rest[i, :, wide] = rest[i, :, wide] - contract(left, found, 1)

    for k in range(blocks):
        step(k)
    xs = [rest[k, :, GROUP * blocks :] for k in range(blocks)]
    for k in range(blocks):
        coeff_ref[GROUP * k : GROUP * k + GROUP, :] = xs[k]
    width = cent_ref.shape[1]
    for piece in range(width // GROUP):
        total = jnp.zeros((ROWS, GROUP), jnp.float32)
        for k in range(blocks):
            values = cent_ref[
                GROUP * k : GROUP * k + GROUP, GROUP * piece : GROUP * piece + GROUP
            ].astype(jnp.float32)
            scaled = values * xs[k]
            total = total + jnp.sum(scaled.reshape(PANELS, ROWS, GROUP), axis=0)
        update_ref[:, GROUP * piece : GROUP * piece + GROUP] = jnp.sum(
            total, axis=0, keepdims=True
        )


VMEM = pl.BlockSpec(memory_space=pltpu.VMEM)
SMEM = pl.BlockSpec(memory_space=pltpu.SMEM)


def center_gram(place, energies, parts):
    columns = parts[0].shape[1]
    return pl.pallas_call(
        center_gram_kernel,
        out_shape=(
            jax.ShapeDtypeStruct((BLOCKS * GROUP, columns), jnp.bfloat16),
            jax.ShapeDtypeStruct((HELD * GROUP, GROUP), jnp.float32),
        ),
        in_specs=[SMEM] + [VMEM] * 5,
        out_specs=(VMEM, VMEM),
        compiler_params=pltpu.CompilerParams(vmem_limit_bytes=32 * 1024 * 1024),
        name="center_gram",
    )(place, energies, *parts)


def solve(blocks, cent):
    return pl.pallas_call(
        solve_kernel,
        out_shape=(
            jax.ShapeDtypeStruct((BLOCKS * GROUP, GROUP), jnp.float32),
            jax.ShapeDtypeStruct((1, cent.shape[1]), jnp.float32),
        ),
        in_specs=[VMEM] * 2,
        out_specs=(VMEM, VMEM),
        scratch_shapes=[
            pltpu.VMEM((BLOCKS, GROUP, (BLOCKS + 1) * GROUP), jnp.float32),
            pltpu.VMEM((BLOCKS, GROUP, (BLOCKS + 1) * GROUP), jnp.float32),
        ],
        compiler_params=pltpu.CompilerParams(vmem_limit_bytes=32 * 1024 * 1024),
        name="solve",
    )(blocks, cent)


SWAP = [(0, 1), (1, 0)]


def per_device(jacobian, energies):
    high = lax.axis_index("high")
    core = lax.axis_index("core")
    half = jacobian.shape[1] // 2
    send = lax.dynamic_slice_in_dim(jacobian, (1 - high) * half, half, 1)
    send, jacobian = lax.optimization_barrier((send, jacobian))
    keep = lax.dynamic_slice_in_dim(jacobian, high * half, half, 1)
    far = lax.ppermute(send, "high", SWAP)
    near = lax.ppermute(keep, "core", SWAP)
    diagonal = lax.ppermute(far, "core", SWAP)
    place = jnp.stack(
        [
            2 * high + core,
            2 * (1 - high) + core,
            2 * high + 1 - core,
            2 * (1 - high) + 1 - core,
            core,
            high,
            lax.axis_index(("z", "x", "low")),
        ]
    ).astype(jnp.int32)
    spread = jnp.broadcast_to(energies[:, None], (GROUP, GROUP))
    cent, partial = center_gram(place, spread, (keep, far, near, diagonal))
    plane = ("high", "x", "low")
    peers = lax.axis_size(plane)
    parts = lax.all_to_all(
        partial.reshape(peers, -1, GROUP), plane, split_axis=0, concat_axis=0, tiled=True
    )
    chunk = jnp.sum(parts, axis=0)
    ring = lax.axis_size("z")
    one, two, three = (
        lax.ppermute(chunk, "z", [(n, (n + step) % ring) for n in range(ring)])
        for step in range(1, ring)
    )
    chunk = (chunk + two) + (one + three)
    everyone = ("core",) + plane
    blocks = lax.all_to_all(
        jnp.broadcast_to(chunk[None], (lax.axis_size(everyone), *chunk.shape)),
        everyone,
        split_axis=0,
        concat_axis=0,
        tiled=True,
    ).reshape(2 * HELD * GROUP, GROUP)
    coeffs, update = solve(blocks, cent)
    own = lax.dynamic_slice_in_dim(coeffs, (2 * high + core) * GROUP, GROUP, 0)[:, 0]
    update = update[0] * math.sqrt(2 * half * lax.axis_size(("z", "x", "low")))
    away = lax.ppermute(update, "high", SWAP)
    lower = jnp.where(high == 0, update, away)
    upper = jnp.where(high == 0, away, update)
    return jnp.concatenate([lower, upper]), own


def solution(mesh):
    fine = Mesh(mesh.devices.reshape(2, 2, 4, 4, 2), ("high", "core", "z", "x", "low"))
    samples, params = ("high", "core"), ("z", "x", "low")
    return jax.shard_map(
        per_device,
        mesh=fine,
        in_specs=(P(samples, params), P(samples)),
        out_specs=(P(params), P(samples)),
        check_vma=False,
    )
```

```python
import math

import jax
import jax.numpy as jnp
from jax import lax
from jax.experimental import pallas as pl
from jax.experimental.pallas import tpu as pltpu
from jax.sharding import Mesh, PartitionSpec as P

GROUP = 128
ROWS = 8
WIDE = 2
PANELS = GROUP // ROWS
RIDGE = 0.05


BLOCKS = 4
STRIPS = (((0, 0, 4), (1, 1, 1)), ((1, 2, 2), (2, 2, 2), (3, 3, 1)))
LISTS = tuple(tuple((r, c + n) for r, c, w in strips for n in range(w)) for strips in STRIPS)
HELD = len(LISTS[0])
SPARE, SPAN = GROUP // 2, 16


def center_gram_kernel(e_ref, a_ref, b_ref, c_ref, d_ref, cent_ref, out_ref):
    total = BLOCKS * GROUP
    scale = 1.0 / math.sqrt(total)
    parts = (a_ref, b_ref, c_ref, d_ref)
    high, core = lax.axis_index("high"), lax.axis_index("core")
    groups = (
        2 * high + core,
        2 * (1 - high) + core,
        2 * high + 1 - core,
        2 * (1 - high) + 1 - core,
    )
    sums = [jnp.sum(part[...].astype(jnp.float32), axis=0, keepdims=True) for part in parts]
    mean = ((sums[0] + sums[2]) + (sums[1] + sums[3])) / total
    for number, part in enumerate(parts):
        start = pl.multiple_of(groups[number] * GROUP, GROUP)
        cent_ref[pl.ds(start, GROUP), :] = (
            (part[...].astype(jnp.float32) - mean) * scale
        ).astype(jnp.bfloat16)
    first_slab = lax.axis_index(("z", "x", "low")) == 0
    for half, strips in enumerate(STRIPS):

        @pl.when(core == half)
        def _():
            at = 0
            for r, c, wide in strips:
                strip = lax.dot_general(
                    cent_ref[GROUP * r : GROUP * r + GROUP, :],
                    cent_ref[GROUP * c : GROUP * (c + wide), :],
                    (((1,), (1,)), ((), ())),
                    preferred_element_type=jnp.float32,
                )
                for n in range(wide):
                    out_ref[at : at + GROUP, :] = strip[:, GROUP * n : GROUP * n + GROUP]
                    at += GROUP

            column = lax.broadcasted_iota(jnp.int32, (SPARE, GROUP), 1)
            pair = jnp.where(column < SPAN, e_ref[:SPARE, :], e_ref[SPARE:, :])
            diagonals = [n for n, (r, c) in enumerate(LISTS[half]) if r == c]
            for group, n in enumerate(diagonals):
                mine = (high == group) & first_slab
                rows = slice(GROUP * n + SPARE, GROUP * (n + 1))
                out_ref[rows, :] = jnp.where(
                    column < 2 * SPAN, jnp.where(mine, pair, 0.0), out_ref[rows, :]
                )


def lane(value, index):
    return jnp.broadcast_to(value[:, index : index + 1], (ROWS, GROUP))


def row(value, index):
    return jnp.broadcast_to(value[index : index + 1, :], (ROWS, GROUP))


def factor_block(rows):
    rows = list(rows)
    column = lax.broadcasted_iota(jnp.int32, (ROWS, GROUP), 1)
    line = lax.broadcasted_iota(jnp.int32, (ROWS, GROUP), 0)
    size = WIDE * ROWS
    inverse, recips = [], []
    for p in range(0, PANELS, WIDE):
        first = ROWS * p
        after = list(range(p + WIDE, min(p + 2 * WIDE, PANELS)))
        beyond = list(range(p + 2 * WIDE, PANELS))
        own = (column >= first) & (column < first + size)
        held = {
            (m, t): lane(rows[p + t], first + m) for m in range(size) for t in range(m // ROWS, WIDE)
        }
        next_held = {(m, i): lane(rows[i], first + m) for m in range(size) for i in after}
        work = [
            jnp.where(own, (column - first - ROWS * t == line).astype(jnp.float32), rows[p + t])
            for t in range(WIDE)
        ]
        following = {i: jnp.where(own, 0.0, rows[i]) for i in after}
        scale = [None] * WIDE
        for j in range(size):
            home, at = divmod(j, ROWS)
            pivot_row = row(work[home], at)
            spread = {m: row(held[j, m // ROWS], m % ROWS) for m in range(j, size)}
            recip = 1.0 / spread[j]
            scale[home] = recip if at == 0 else jnp.where(line == at, recip, scale[home])
            factor = {t: held[j, t] * recip for t in range(home, WIDE)}
            for m in range(j + 1, size):
                for t in range(m // ROWS, WIDE):
                    held[m, t] = held[m, t] - factor[t] * spread[m]
            for t in range(home, WIDE):
                change = work[t] - factor[t] * pivot_row
                work[t] = jnp.where(line > at, change, work[t]) if t == home else change
            for i in after:
                part = next_held[j, i] * recip
                for m in range(j + 1, size):
                    next_held[m, i] = next_held[m, i] - part * spread[m]
                following[i] = following[i] - part * pivot_row
        for t in range(WIDE):
            inverse.append(jnp.where(column < first + size, work[t], 0.0))
            recips.append(scale[t])
        for i in after:
            rows[i] = following[i]
        if beyond:
            panel = jnp.concatenate(work, axis=0)
            scaled = jnp.concatenate([work[t] * scale[t] for t in range(WIDE)], axis=0)
            change = contract(stack_left(scaled, 0), stack_right(panel, 0), 0)
            for i in beyond:
                change_tile = change[ROWS * i : ROWS * i + ROWS, :]
                rows[i] = jnp.where(own, 0.0, rows[i]) - change_tile
    return inverse, recips


def split(value):
    high = value.astype(jnp.bfloat16)
    rest = value - high.astype(jnp.float32)
    middle = rest.astype(jnp.bfloat16)
    return high, middle, (rest - middle.astype(jnp.float32)).astype(jnp.bfloat16)


def stack_left(value, axis):
    high, middle, low = split(value)
    return jnp.concatenate([high, high, middle, middle, high, low], axis=axis)


def stack_right(value, axis):
    high, middle, low = split(value)
    return jnp.concatenate([high, middle, high, middle, low, high], axis=axis)


def contract(left, right, axis):
    return lax.dot_general(
        left, right, (((axis,), (0,)), ((), ())), preferred_element_type=jnp.float32
    )


def solve_kernel(
    mine_ref, other_ref, cent_ref, coeff_ref, update_ref, parts, gram, rest
):
    blocks = BLOCKS
    core = lax.axis_index("core")
    parts[core] = mine_ref[...]
    parts[1 - core] = other_ref[...]
    for core, held in enumerate(LISTS):
        for n, (r, c) in enumerate(held):
            gram[r, :, GROUP * c : GROUP * c + GROUP] = parts[
                core, GROUP * n : GROUP * n + GROUP, :
            ]
    energy_sum = jnp.zeros((ROWS, GROUP), jnp.float32)
    for core, held in enumerate(LISTS):
        for high, k in enumerate(r for r, c in held if r == c):
            for p in range(PANELS):
                which, start = divmod(ROWS * p, SPARE)
                tile = gram[
                    k, SPARE + start : SPARE + start + ROWS, GROUP * k : GROUP * k + GROUP
                ]
                value = lane(tile, SPAN * which)
                gram[2 * high + core, ROWS * p : ROWS * p + ROWS, GROUP * blocks :] = value
                energy_sum = energy_sum + value
    energy_mean = jnp.sum(energy_sum, axis=0, keepdims=True) / (blocks * GROUP)
    scale = 1.0 / math.sqrt(blocks * GROUP)
    for k in range(blocks):
        gram[k, :, GROUP * blocks :] = (gram[k, :, GROUP * blocks :] - energy_mean) * scale
    column = lax.broadcasted_iota(jnp.int32, (ROWS, GROUP), 1)
    line = lax.broadcasted_iota(jnp.int32, (ROWS, GROUP), 0)

    def step(k):
        panels = []
        for p in range(PANELS):
            ridge = jnp.where(column - ROWS * p == line, RIDGE, 0.0)
            tile = gram[k, ROWS * p : ROWS * p + ROWS, GROUP * k : GROUP * k + GROUP]
            panels.append(tile + ridge)
        inverse, recips = factor_block(panels)
        triangle = jnp.concatenate(inverse, axis=0)
        tri = stack_left(triangle, 1)
        tri_turned = stack_left(triangle, 0)
        wide = slice(GROUP * (k + 1), GROUP * (blocks + 1))
        y = contract(tri, stack_right(gram[k, :, wide], 0), 1)
        inverse_d = jnp.concatenate(recips, axis=0)
        right = stack_right(y * jnp.concatenate([inverse_d] * (blocks - k), axis=1), 0)
        for i in range(k + 1, blocks):
            skip = GROUP * (i - k - 1)
            left = stack_left(y[:, skip : skip + GROUP], 0)
            place = slice(GROUP * i, GROUP * (blocks + 1))
            gram[i, :, place] = gram[i, :, place] - contract(left, right[:, skip:], 0)
        rest[k, :, wide] = contract(tri_turned, right, 0)
        if k:
            found = stack_right(rest[k, :, wide], 0)
        for i in range(k):
            left = stack_left(rest[i, :, GROUP * k : GROUP * k + GROUP], 1)
            rest[i, :, wide] = rest[i, :, wide] - contract(left, found, 1)

    for k in range(blocks):
        step(k)
    xs = [rest[k, :, GROUP * blocks :] for k in range(blocks)]
    for k in range(blocks):
        coeff_ref[GROUP * k : GROUP * k + GROUP, :] = xs[k]
    width = cent_ref.shape[1]
    for piece in range(width // GROUP):
        total = jnp.zeros((ROWS, GROUP), jnp.float32)
        for k in range(blocks):
            values = cent_ref[
                GROUP * k : GROUP * k + GROUP, GROUP * piece : GROUP * piece + GROUP
            ].astype(jnp.float32)
            scaled = values * xs[k]
            total = total + jnp.sum(scaled.reshape(PANELS, ROWS, GROUP), axis=0)
        update_ref[:, GROUP * piece : GROUP * piece + GROUP] = jnp.sum(
            total, axis=0, keepdims=True
        )


VMEM = pl.BlockSpec(memory_space=pltpu.VMEM)


def center_gram(energies, parts):
    columns = parts[0].shape[1]
    return pl.pallas_call(
        center_gram_kernel,
        out_shape=(
            jax.ShapeDtypeStruct((BLOCKS * GROUP, columns), jnp.bfloat16),
            jax.ShapeDtypeStruct((HELD * GROUP, GROUP), jnp.float32),
        ),
        in_specs=[VMEM] * 5,
        out_specs=(VMEM, VMEM),
        compiler_params=pltpu.CompilerParams(vmem_limit_bytes=32 * 1024 * 1024),
        name="center_gram",
    )(energies, *parts)


def solve(mine, other, cent):
    return pl.pallas_call(
        solve_kernel,
        out_shape=(
            jax.ShapeDtypeStruct((BLOCKS * GROUP, GROUP), jnp.float32),
            jax.ShapeDtypeStruct((1, cent.shape[1]), jnp.float32),
        ),
        in_specs=[VMEM] * 3,
        out_specs=(VMEM, VMEM),
        scratch_shapes=[
            pltpu.VMEM((2, HELD * GROUP, GROUP), jnp.float32),
            pltpu.VMEM((BLOCKS, GROUP, (BLOCKS + 1) * GROUP), jnp.float32),
            pltpu.VMEM((BLOCKS, GROUP, (BLOCKS + 1) * GROUP), jnp.float32),
        ],
        compiler_params=pltpu.CompilerParams(vmem_limit_bytes=32 * 1024 * 1024),
        name="solve",
    )(mine, other, cent)


SWAP = [(0, 1), (1, 0)]


def per_device(jacobian, energies):
    high = lax.axis_index("high")
    core = lax.axis_index("core")
    half = jacobian.shape[1] // 2
    send = lax.dynamic_slice_in_dim(jacobian, (1 - high) * half, half, 1)
    send, jacobian = lax.optimization_barrier((send, jacobian))
    keep = lax.dynamic_slice_in_dim(jacobian, high * half, half, 1)
    far = lax.ppermute(send, "high", SWAP)
    near = lax.ppermute(keep, "core", SWAP)
    diagonal = lax.ppermute(far, "core", SWAP)
    spread = jnp.broadcast_to(energies[:, None], (GROUP, GROUP))
    cent, partial = center_gram(spread, (keep, far, near, diagonal))
    plane = ("high", "x", "low")
    peers = lax.axis_size(plane)
    parts = lax.all_to_all(
        partial.reshape(peers, -1, GROUP), plane, split_axis=0, concat_axis=0, tiled=True
    )
    chunk = jnp.sum(parts, axis=0)
    ring = lax.axis_size("z")
    one, two, three = (
        lax.ppermute(chunk, "z", [(n, (n + step) % ring) for n in range(ring)])
        for step in range(1, ring)
    )
    chunk = (chunk + two) + (one + three)
    mine = lax.all_to_all(
        jnp.broadcast_to(chunk[None], (peers, *chunk.shape)),
        plane,
        split_axis=0,
        concat_axis=0,
        tiled=True,
    ).reshape(HELD * GROUP, GROUP)
    other = lax.ppermute(mine, "core", SWAP)
    coeffs, update = solve(mine, other, cent)
    own = lax.dynamic_slice_in_dim(coeffs, (2 * high + core) * GROUP, GROUP, 0)[:, 0]
    update = update[0] * math.sqrt(2 * half * lax.axis_size(("z", "x", "low")))
    away = lax.ppermute(update, "high", SWAP)
    lower = jnp.where(high == 0, update, away)
    upper = jnp.where(high == 0, away, update)
    return jnp.concatenate([lower, upper]), own


def solution(mesh):
    fine = Mesh(mesh.devices.reshape(2, 2, 4, 4, 2), ("high", "core", "z", "x", "low"))
    samples, params = ("high", "core"), ("z", "x", "low")
    return jax.shard_map(
        per_device,
        mesh=fine,
        in_specs=(P(samples, params), P(samples)),
        out_specs=(P(params), P(samples)),
        check_vma=False,
    )
```

```python
import math

import jax
import jax.numpy as jnp
from jax import lax
from jax.experimental import pallas as pl
from jax.experimental.pallas import tpu as pltpu
from jax.sharding import Mesh, PartitionSpec as P

GROUP = 128
ROWS = 8
WIDE = 2
PANELS = GROUP // ROWS
RIDGE = 0.05


BLOCKS = 4
STRIPS = (((0, 0, 4), (1, 1, 1)), ((1, 2, 2), (2, 2, 2), (3, 3, 1)))
LISTS = tuple(tuple((r, c + n) for r, c, w in strips for n in range(w)) for strips in STRIPS)
HELD = len(LISTS[0])
SPARE, SPAN = GROUP // 2, 16


def center_gram_kernel(e_ref, a_ref, b_ref, c_ref, d_ref, cent_ref, out_ref):
    total = BLOCKS * GROUP
    scale = 1.0 / math.sqrt(total)
    parts = (a_ref, b_ref, c_ref, d_ref)
    high, core = lax.axis_index("high"), lax.axis_index("core")
    groups = (
        2 * high + core,
        2 * (1 - high) + core,
        2 * high + 1 - core,
        2 * (1 - high) + 1 - core,
    )
    sums = [jnp.sum(part[...].astype(jnp.float32), axis=0, keepdims=True) for part in parts]
    mean = ((sums[0] + sums[2]) + (sums[1] + sums[3])) / total
    for number, part in enumerate(parts):
        start = pl.multiple_of(groups[number] * GROUP, GROUP)
        cent_ref[pl.ds(start, GROUP), :] = (
            (part[...].astype(jnp.float32) - mean) * scale
        ).astype(jnp.bfloat16)
    first_slab = lax.axis_index(("z", "x", "low")) == 0
    for half, strips in enumerate(STRIPS):

        @pl.when(core == half)
        def _():
            at = 0
            for r, c, wide in strips:
                strip = lax.dot_general(
                    cent_ref[GROUP * r : GROUP * r + GROUP, :],
                    cent_ref[GROUP * c : GROUP * (c + wide), :],
                    (((1,), (1,)), ((), ())),
                    preferred_element_type=jnp.float32,
                )
                for n in range(wide):
                    out_ref[at : at + GROUP, :] = strip[:, GROUP * n : GROUP * n + GROUP]
                    at += GROUP

            column = lax.broadcasted_iota(jnp.int32, (SPARE, GROUP), 1)
            pair = jnp.where(column < SPAN, e_ref[:SPARE, :], e_ref[SPARE:, :])
            diagonals = [n for n, (r, c) in enumerate(LISTS[half]) if r == c]
            for group, n in enumerate(diagonals):
                mine = (high == group) & first_slab
                rows = slice(GROUP * n + SPARE, GROUP * (n + 1))
                out_ref[rows, :] = jnp.where(
                    column < 2 * SPAN, jnp.where(mine, pair, 0.0), out_ref[rows, :]
                )


def lane(value, index):
    return jnp.broadcast_to(value[:, index : index + 1], (ROWS, GROUP))


def row(value, index):
    return jnp.broadcast_to(value[index : index + 1, :], (ROWS, GROUP))


def factor_block(rows):
    rows = list(rows)
    column = lax.broadcasted_iota(jnp.int32, (ROWS, GROUP), 1)
    line = lax.broadcasted_iota(jnp.int32, (ROWS, GROUP), 0)
    size = WIDE * ROWS
    inverse, recips = [], []
    for p in range(0, PANELS, WIDE):
        first = ROWS * p
        after = list(range(p + WIDE, min(p + 2 * WIDE, PANELS)))
        beyond = list(range(p + 2 * WIDE, PANELS))
        own = (column >= first) & (column < first + size)
        held = {
            (m, t): lane(rows[p + t], first + m) for m in range(size) for t in range(m // ROWS, WIDE)
        }
        next_held = {(m, i): lane(rows[i], first + m) for m in range(size) for i in after}
        work = [
            jnp.where(own, (column - first - ROWS * t == line).astype(jnp.float32), rows[p + t])
            for t in range(WIDE)
        ]
        following = {i: jnp.where(own, 0.0, rows[i]) for i in after}
        scale = [None] * WIDE
        for j in range(size):
            home, at = divmod(j, ROWS)
            pivot_row = row(work[home], at)
            spread = {m: row(held[j, m // ROWS], m % ROWS) for m in range(j, size)}
            recip = 1.0 / spread[j]
            scale[home] = recip if at == 0 else jnp.where(line == at, recip, scale[home])
            factor = {t: held[j, t] * recip for t in range(home, WIDE)}
            for m in range(j + 1, size):
                for t in range(m // ROWS, WIDE):
                    held[m, t] = held[m, t] - factor[t] * spread[m]
            for t in range(home, WIDE):
                change = work[t] - factor[t] * pivot_row
                work[t] = jnp.where(line > at, change, work[t]) if t == home else change
            for i in after:
                part = next_held[j, i] * recip
                for m in range(j + 1, size):
                    next_held[m, i] = next_held[m, i] - part * spread[m]
                following[i] = following[i] - part * pivot_row
        for t in range(WIDE):
            inverse.append(jnp.where(column < first + size, work[t], 0.0))
            recips.append(scale[t])
        for i in after:
            rows[i] = following[i]
        if beyond:
            panel = jnp.concatenate(work, axis=0)
            scaled = jnp.concatenate([work[t] * scale[t] for t in range(WIDE)], axis=0)
            change = contract(stack_left(scaled, 0), stack_right(panel, 0), 0)
            for i in beyond:
                change_tile = change[ROWS * i : ROWS * i + ROWS, :]
                rows[i] = jnp.where(own, 0.0, rows[i]) - change_tile
    return inverse, recips


def split(value):
    high = value.astype(jnp.bfloat16)
    rest = value - high.astype(jnp.float32)
    middle = rest.astype(jnp.bfloat16)
    return high, middle, (rest - middle.astype(jnp.float32)).astype(jnp.bfloat16)


def stack_left(value, axis):
    high, middle, low = split(value)
    return jnp.concatenate([high, high, middle, middle, high, low], axis=axis)


def stack_right(value, axis):
    high, middle, low = split(value)
    return jnp.concatenate([high, middle, high, middle, low, high], axis=axis)


def contract(left, right, axis):
    return lax.dot_general(
        left, right, (((axis,), (0,)), ((), ())), preferred_element_type=jnp.float32
    )


def solve_kernel(
    mine_ref, other_ref, cent_ref, coeff_ref, update_ref, parts, gram, rest
):
    blocks = BLOCKS
    core_index = lax.axis_index("core")
    parts[core_index] = mine_ref[...]
    parts[1 - core_index] = other_ref[...]
    for core, held in enumerate(LISTS):
        for n, (r, c) in enumerate(held):
            gram[r, :, GROUP * c : GROUP * c + GROUP] = parts[
                core, GROUP * n : GROUP * n + GROUP, :
            ]
    energy_sum = jnp.zeros((ROWS, GROUP), jnp.float32)
    for core, held in enumerate(LISTS):
        for high, k in enumerate(r for r, c in held if r == c):
            for p in range(PANELS):
                which, start = divmod(ROWS * p, SPARE)
                tile = gram[
                    k, SPARE + start : SPARE + start + ROWS, GROUP * k : GROUP * k + GROUP
                ]
                value = lane(tile, SPAN * which)
                gram[2 * high + core, ROWS * p : ROWS * p + ROWS, GROUP * blocks :] = value
                energy_sum = energy_sum + value
    energy_mean = jnp.sum(energy_sum, axis=0, keepdims=True) / (blocks * GROUP)
    scale = 1.0 / math.sqrt(blocks * GROUP)
    for k in range(blocks):
        gram[k, :, GROUP * blocks :] = (gram[k, :, GROUP * blocks :] - energy_mean) * scale
    column = lax.broadcasted_iota(jnp.int32, (ROWS, GROUP), 1)
    line = lax.broadcasted_iota(jnp.int32, (ROWS, GROUP), 0)

    def step(k):
        panels = []
        for p in range(PANELS):
            ridge = jnp.where(column - ROWS * p == line, RIDGE, 0.0)
            tile = gram[k, ROWS * p : ROWS * p + ROWS, GROUP * k : GROUP * k + GROUP]
            panels.append(tile + ridge)
        inverse, recips = factor_block(panels)
        triangle = jnp.concatenate(inverse, axis=0)
        tri = stack_left(triangle, 1)
        tri_turned = stack_left(triangle, 0)
        wide = slice(GROUP * (k + 1), GROUP * (blocks + 1))
        y = contract(tri, stack_right(gram[k, :, wide], 0), 1)
        inverse_d = jnp.concatenate(recips, axis=0)
        right = stack_right(y * jnp.concatenate([inverse_d] * (blocks - k), axis=1), 0)
        for i in range(k + 1, blocks):
            skip = GROUP * (i - k - 1)
            left = stack_left(y[:, skip : skip + GROUP], 0)
            place = slice(GROUP * i, GROUP * (blocks + 1))
            gram[i, :, place] = gram[i, :, place] - contract(left, right[:, skip:], 0)
        rest[k, :, wide] = contract(tri_turned, right, 0)
        if k:
            found = stack_right(rest[k, :, wide], 0)
        for i in range(k):
            left = stack_left(rest[i, :, GROUP * k : GROUP * k + GROUP], 1)
            rest[i, :, wide] = rest[i, :, wide] - contract(left, found, 1)

    for k in range(blocks):
        step(k)
    xs = [rest[k, :, GROUP * blocks :] for k in range(blocks)]
    mine = 2 * lax.axis_index("high") + core_index
    coeff_ref[...] = rest[mine, :, GROUP * blocks :]
    width = cent_ref.shape[1]
    for piece in range(width // GROUP):
        total = jnp.zeros((ROWS, GROUP), jnp.float32)
        for k in range(blocks):
            values = cent_ref[
                GROUP * k : GROUP * k + GROUP, GROUP * piece : GROUP * piece + GROUP
            ].astype(jnp.float32)
            scaled = values * xs[k]
            total = total + jnp.sum(scaled.reshape(PANELS, ROWS, GROUP), axis=0)
        update_ref[:, GROUP * piece : GROUP * piece + GROUP] = jnp.sum(
            total, axis=0, keepdims=True
        )


VMEM = pl.BlockSpec(memory_space=pltpu.VMEM)


def center_gram(energies, parts):
    columns = parts[0].shape[1]
    return pl.pallas_call(
        center_gram_kernel,
        out_shape=(
            jax.ShapeDtypeStruct((BLOCKS * GROUP, columns), jnp.bfloat16),
            jax.ShapeDtypeStruct((HELD * GROUP, GROUP), jnp.float32),
        ),
        in_specs=[VMEM] * 5,
        out_specs=(VMEM, VMEM),
        compiler_params=pltpu.CompilerParams(vmem_limit_bytes=32 * 1024 * 1024),
        name="center_gram",
    )(energies, *parts)


def solve(mine, other, cent):
    return pl.pallas_call(
        solve_kernel,
        out_shape=(
            jax.ShapeDtypeStruct((GROUP, GROUP), jnp.float32),
            jax.ShapeDtypeStruct((1, cent.shape[1]), jnp.float32),
        ),
        in_specs=[VMEM] * 3,
        out_specs=(VMEM, VMEM),
        scratch_shapes=[
            pltpu.VMEM((2, HELD * GROUP, GROUP), jnp.float32),
            pltpu.VMEM((BLOCKS, GROUP, (BLOCKS + 1) * GROUP), jnp.float32),
            pltpu.VMEM((BLOCKS, GROUP, (BLOCKS + 1) * GROUP), jnp.float32),
        ],
        compiler_params=pltpu.CompilerParams(vmem_limit_bytes=32 * 1024 * 1024),
        name="solve",
    )(mine, other, cent)


SWAP = [(0, 1), (1, 0)]


def per_device(jacobian, energies):
    high = lax.axis_index("high")
    core = lax.axis_index("core")
    half = jacobian.shape[1] // 2
    send = lax.dynamic_slice_in_dim(jacobian, (1 - high) * half, half, 1)
    send, jacobian = lax.optimization_barrier((send, jacobian))
    keep = lax.dynamic_slice_in_dim(jacobian, high * half, half, 1)
    far = lax.ppermute(send, "high", SWAP)
    near = lax.ppermute(keep, "core", SWAP)
    diagonal = lax.ppermute(far, "core", SWAP)
    spread = jnp.broadcast_to(energies[:, None], (GROUP, GROUP))
    cent, partial = center_gram(spread, (keep, far, near, diagonal))
    plane = ("high", "x", "low")
    peers = lax.axis_size(plane)
    parts = lax.all_to_all(
        partial.reshape(peers, -1, GROUP), plane, split_axis=0, concat_axis=0, tiled=True
    )
    chunk = jnp.sum(parts, axis=0)
    ring = lax.axis_size("z")
    one, two, three = (
        lax.ppermute(chunk, "z", [(n, (n + step) % ring) for n in range(ring)])
        for step in range(1, ring)
    )
    chunk = (chunk + two) + (one + three)
    mine = lax.all_to_all(
        jnp.broadcast_to(chunk[None], (peers, *chunk.shape)),
        plane,
        split_axis=0,
        concat_axis=0,
        tiled=True,
    ).reshape(HELD * GROUP, GROUP)
    other = lax.ppermute(mine, "core", SWAP)
    coeffs, update = solve(mine, other, cent)
    own = coeffs[:, 0]
    update = update[0] * math.sqrt(2 * half * lax.axis_size(("z", "x", "low")))
    away = lax.ppermute(update, "high", SWAP)
    whole = lax.dynamic_update_slice(jnp.zeros((2 * half,), jnp.float32), update, (high * half,))
    return lax.dynamic_update_slice(whole, away, ((1 - high) * half,)), own


def solution(mesh):
    fine = Mesh(mesh.devices.reshape(2, 2, 4, 4, 2), ("high", "core", "z", "x", "low"))
    samples, params = ("high", "core"), ("z", "x", "low")
    return jax.shard_map(
        per_device,
        mesh=fine,
        in_specs=(P(samples, params), P(samples)),
        out_specs=(P(params), P(samples)),
        check_vma=False,
    )
```
